32 devices in a mesh: path: 8 (over y, x, core), shard: 4 (over z).
Axes of the slice: x: 2, y: 2, z: 4, core: 2. Of those that a mesh axis runs over, the one named last changes fastest.
Arguments:
- path_params: bfloat16 [8, 16, 32, 4096], P('path', None, 'shard'), may hold values from -6 to 6
- global_params: float32 [128, 32, 4096], P('path', 'shard'), may hold values from -6 to 6
- momentum: float32 [128, 32, 4096], P('path', 'shard'), may hold values from -6 to 6
- module_ids: int32 [8, 16], replicated, may hold values from 0 to 127, as said below
- token_counts: int32 [8, 16], replicated, may hold values from 16 to 256
Outputs:
- new_global: float32 [128, 32, 4096], P('path', 'shard')
- new_momentum: float32 [128, 32, 4096], P('path', 'shard')
- path_modules: bfloat16 [8, 16, 32, 4096], P('path', None, 'shard')
The draws below stay inside these ranges and needn't reach their ends.
Inputs may be any that keep to these rules, and one draw needn't show every extreme that they name: `module_ids`: each row names 16 different modules. Among the modules of one row, at most 2 lie in any one block of 16 consecutive module numbers, and every row has exactly 2 in some block.
All inputs are finite; a program needn't handle non-finite values.
Results may differ from the reference program's by a relative error of at most 0.0004.
Values may be sent and summed in bfloat16 or wider, within the bound.
No kernel may reach another device: no remote copies, remote signals or barrier semaphores. Data moves between devices by JAX's collectives and lax.ppermute only.
A program may use at most 128 MiB of HBM per device.

```python
import jax
import jax.numpy as jnp
from jax import lax

D = 4096
OWNED = 16
HELD = 16
PATHS = 8
MODULES = 128
ROWS = 32


def draw_module_ids(key, part):
    base = jax.random.fold_in(key, 11)
    popular = jax.random.randint(jax.random.fold_in(base, 1), (PATHS, OWNED), 0, 4)

    def one_path(index):
        path_key = jax.random.fold_in(base, 100 + index)
        pool = jnp.arange(2 * PATHS, dtype=jnp.int32) % PATHS
        chosen = jax.random.permutation(jax.random.fold_in(path_key, 1), pool)[:HELD]
        first_count = jnp.sum((chosen[:HELD - 1] == chosen[0]).astype(jnp.int32))
        last = jnp.where(first_count == 1, chosen[0], chosen[HELD - 1])
        chosen = chosen.at[HELD - 1].set(last)
        places = jnp.arange(HELD, dtype=jnp.int32)
        before = (chosen[None, :] == chosen[:, None]) & (places[None, :] < places[:, None])
        earlier = jnp.sum(before.astype(jnp.int32), axis=1)
        noise = jax.random.randint(jax.random.fold_in(path_key, 2), (PATHS, OWNED), 0, 1024)
        scores = (noise + popular * 1024) * OWNED + jnp.arange(OWNED, dtype=jnp.int32)[None, :]
        order = jnp.argsort(-scores, axis=1, stable=True).astype(jnp.int32)
        local = order[chosen, earlier]
        return (chosen * OWNED + local).astype(jnp.int32)
    return jax.vmap(one_path)(jnp.arange(PATHS, dtype=jnp.int32))


def place_ends(entries, rng, smallest, largest):
    dims = entries.shape
    spot = [jax.random.randint(jax.random.fold_in(rng, axis), (), 0, dims[axis]) for axis in range(len(dims))]
    entries = entries.at[tuple(spot)].set(smallest)
    longest = dims.index(max(dims))
    spot[longest] = (spot[longest] + 1) % dims[longest]
    return entries.at[tuple(spot)].set(largest)


def shard_levels(rng, extent, pieces, low, largest):
    gain = 1.0
    for axis_at, blocks in pieces:
        draws = jax.random.uniform(jax.random.fold_in(jax.random.fold_in(rng, 6), axis_at), (blocks,), jnp.float32, low / len(pieces), largest / len(pieces))
        gain = gain * jnp.repeat(jnp.exp(draws), extent[axis_at] // blocks).reshape((-1,) + (1,) * (len(extent) - 1 - axis_at))
    return gain


def gaussian(own_key, dims, width, limit, split=(), kind=jnp.bfloat16):
    drawn = width * jax.random.normal(own_key, dims, jnp.float32)
    if split:
        drawn = drawn * shard_levels(own_key, dims, split, -0.22, 0.18)
    return jnp.clip(drawn, -limit, limit).astype(kind)


def setup_inputs(seed: int = 0) -> dict:
    splits = jax.random.split(jax.random.key(seed), 6)
    path_params = gaussian(splits[0], (PATHS, HELD, ROWS, D), 1.0, 6.0, ((0, 8), (2, 4)))
    global_params = gaussian(splits[1], (MODULES, ROWS, D), 1.0, 6.0, ((0, 8), (1, 4)), jnp.float32)
    momentum = gaussian(splits[2], (MODULES, ROWS, D), 1.0, 6.0, ((0, 8), (1, 4)), jnp.float32)
    module_ids = draw_module_ids(jax.random.fold_in(splits[5], 71), 0)
    token_counts = place_ends(jax.random.randint(splits[4], (PATHS, HELD), 16, 257), jax.random.fold_in(splits[4], 1), 16, 256).astype(jnp.int32)
    return dict(path_params=path_params, global_params=global_params, momentum=momentum, module_ids=module_ids, token_counts=token_counts)


outer_momentum = 0.9
outer_rate = 0.7

def reference(path_params, global_params, momentum, module_ids, token_counts):
    flat = path_params.reshape(PATHS * HELD, ROWS * D).astype(jnp.float32)
    flat_ids = module_ids.reshape(-1)
    flat_counts = token_counts.reshape(-1).astype(jnp.float32)
    targets = jnp.arange(MODULES, dtype=jnp.int32)
    weights = jnp.where(flat_ids[None, :] == targets[:, None], flat_counts[None, :], jnp.float32(0.0))
    total = lax.optimization_barrier(jnp.sum(weights, axis=1))
    summed = jnp.dot(weights, flat, precision=lax.Precision.HIGHEST)
    params = global_params.reshape(MODULES, ROWS * D)
    past = momentum.reshape(MODULES, ROWS * D)
    raw = (total[:, None] * params - summed) / jnp.maximum(total, 1.0)[:, None]
    factor = jnp.minimum(1.0, 1.0 / jnp.sqrt(lax.optimization_barrier(jnp.mean(raw * raw, axis=1)) + 1e-06))
    delta = raw * factor[:, None]
    velocity = outer_momentum * past + delta
    updated = params - outer_rate * (outer_momentum * velocity + delta)
    rounded = updated.astype(jnp.bfloat16)
    picked = rounded[flat_ids]
    return (updated.reshape(MODULES, ROWS, D), velocity.reshape(MODULES, ROWS, D), picked.reshape(PATHS, HELD, ROWS, D))
```

```python
import functools

import jax
import jax.numpy as jnp
from jax import lax
from jax.experimental import pallas as pl
from jax.experimental.pallas import tpu as pltpu
from jax.sharding import PartitionSpec as P

CAP = 2
CHUNK = 1024
outer_momentum = 0.9
outer_rate = 0.7

SMEM = pl.BlockSpec(memory_space=pltpu.SMEM)
VMEM = pl.BlockSpec(memory_space=pltpu.VMEM)
ANY = pl.BlockSpec(memory_space=pl.ANY)


def in_vmem(x):
    return pltpu.with_memory_space_constraint(x, pltpu.VMEM)


def chunks(width):
    step = CHUNK if width % CHUNK == 0 else width
    return [pl.ds(at, step) for at in range(0, width, step)]


def pack_kernel(paths, owned, me_ref, ids_ref, local_ref, places_ref, *rest):
    pieces, (seen, sems) = rest[:paths], rest[paths:]
    me = me_ref[0]
    held = ids_ref.shape[1]

    def clear(i, _):
        places_ref[i] = jnp.int32(-1)
        return 0

    def reset(i, _):
        seen[i] = jnp.int32(0)
        return 0

    def place(k, _):
        group = ids_ref[me, k] // owned
        rank = seen[group]
        seen[group] = rank + 1
        places_ref[group * CAP + rank] = k
        return 0

    lax.fori_loop(0, paths * CAP, clear, 0)
    lax.fori_loop(0, paths, reset, 0)
    lax.fori_loop(0, held, place, 0)
    copies = []
    for d in list(range(1, paths)) + [0]:
        for r in range(CAP):
            k = jnp.maximum(places_ref[(me ^ d) * CAP + r], 0)
            copy = pltpu.make_async_copy(
                local_ref.at[k], pieces[d].at[r], sems.at[d * CAP + r]
            )
            copy.start()
            copies.append(copy)
    for copy in copies:
        copy.wait()


def early_kernel(
    paths, me_ref, ids_ref, counts_ref, own_ref, params_ref, past_ref,
    module_ref, weight_ref, total_ref, acc_ref, base_ref,
):
    me = me_ref[0]
    owned, _, width = params_ref.shape
    held = ids_ref.shape[1]

    def clear(i, _):
        module_ref[i] = jnp.int32(0)
        weight_ref[i] = jnp.float32(0.0)
        return 0

    def reset(i, _):
        total_ref[i] = jnp.float32(0.0)
        return 0

    lax.fori_loop(0, paths * CAP, clear, 0)
    lax.fori_loop(0, owned, reset, 0)

    def one(i, rank):
        path, k = i // held, i % held
        rank = jnp.where(k == 0, 0, rank)
        at = ids_ref[path, k] - me * owned
        mine = (at >= 0) & (at < owned)

        @pl.when(mine)
        def _():
            count = counts_ref[path, k]
            module_ref[path * CAP + rank] = at
            weight_ref[path * CAP + rank] = count
            total_ref[at] = total_ref[at] + count

        return jnp.where(mine, rank + 1, rank)

    lax.fori_loop(0, paths * held, one, jnp.int32(0))

    def fill(m, _):
        for c in chunks(width):
            params = params_ref[m, :, c]
            acc_ref[m, :, c] = total_ref[m] * params
            base_ref[m, :, c] = params - (outer_rate * outer_momentum**2) * past_ref[m, :, c]
        return 0

    lax.fori_loop(0, owned, fill, 0)
    subtract(me, [own_ref], [0], module_ref, weight_ref, acc_ref)


def subtract(me, pieces, distances, module_ref, weight_ref, acc_ref):
    width = acc_ref.shape[2]
    for piece, d in zip(pieces, distances, strict=True):
        for r in range(CAP):
            slot = (me ^ d) * CAP + r
            m, weight = module_ref[slot], weight_ref[slot]
            for c in chunks(width):
                acc_ref[m, :, c] = acc_ref[m, :, c] - weight * piece[r, :, c].astype(jnp.float32)


def combine_kernel(paths, me_ref, module_ref, weight_ref, total_ref, acc_in, *rest):
    pieces, (acc_ref, squares_ref) = rest[: paths - 1], rest[paths - 1 :]
    subtract(me_ref[0], pieces, range(1, paths), module_ref, weight_ref, acc_ref)
    owned, rows, width = acc_ref.shape
    for m in range(owned):
        inverse = 1.0 / jnp.maximum(jnp.full((rows, 128), total_ref[m], jnp.float32), 1.0)
        added = jnp.zeros((rows, 128), jnp.float32)
        for at in range(0, width, 128):
            raw = acc_ref[m, :, pl.ds(at, 128)] * inverse
            added = added + raw * raw
        squares_ref[pl.ds(m, 1), :] = jnp.sum(added, axis=0, keepdims=True)


def scales(entries, total, squares):
    inverse = 1.0 / jnp.maximum(total, 1.0)
    mean = jnp.sum(squares, axis=1, keepdims=True) / entries
    factor = jnp.minimum(1.0, 1.0 / jnp.sqrt(mean + 1e-06))
    return inverse * factor


def send_kernel(paths, shards, me_ref, module_ref, total_ref, acc_ref, base_ref, *rest):
    squares, (scale_ref, *pieces) = rest[:shards], rest[shards:]
    me = me_ref[0]
    owned, rows, width = acc_ref.shape
    summed = squares[0][...]
    for other in squares[1:]:
        summed = summed + other[...]
    total = jnp.concatenate(
        [jnp.full((1, 128), total_ref[m], jnp.float32) for m in range(owned)], axis=0
    )
    scale = scales(rows * width * shards, total, summed)
    for m in range(owned):
        scale_ref[m] = jnp.broadcast_to(scale[m : m + 1, :], (rows, 128))
    rate = outer_rate * (1.0 + outer_momentum)
    for d in list(range(1, paths)) + [0]:
        for r in range(CAP):
            m = module_ref[(me ^ d) * CAP + r]
            step = rate * scale_ref[m][:, :1]
            for c in chunks(width):
                pieces[d][r, :, c] = (base_ref[m, :, c] - step * acc_ref[m, :, c]).astype(
                    jnp.bfloat16
                )


def store_kernel(scale_ref, acc_ref, base_ref, past_ref, updated_ref, velocity_ref):
    rate = outer_rate * (1.0 + outer_momentum)
    scale = scale_ref[0][:, :1]
    for c in chunks(acc_ref.shape[2]):
        delta = scale * acc_ref[0, :, c]
        updated_ref[0, :, c] = base_ref[0, :, c] - rate * delta
        velocity_ref[0, :, c] = outer_momentum * past_ref[0, :, c] + delta


def unpack_kernel(paths, me_ref, places_ref, *rest):
    pieces, (out_ref, sems) = rest[:paths], rest[paths:]
    me = me_ref[0]
    for wait in (False, True):
        for d in range(paths):
            for r in range(CAP):
                k = places_ref[(me ^ d) * CAP + r]

                @pl.when(k >= 0)
                def _():
                    copy = pltpu.make_async_copy(
                        pieces[d].at[r], out_ref.at[0, k], sems.at[d * CAP + r]
                    )
                    if wait:
                        copy.wait()
                    else:
                        copy.start()


def on_device(path_params, global_params, momentum, module_ids, token_counts):
    paths, held = module_ids.shape
    owned, rows, width = global_params.shape
    shards = lax.axis_size("shard")
    me = lax.axis_index("path").astype(jnp.int32).reshape(1)
    counts = token_counts.astype(jnp.float32)
    slots = paths * CAP
    piece = jax.ShapeDtypeStruct((CAP, rows, width), jnp.bfloat16)
    module = jax.ShapeDtypeStruct((owned, rows, width), jnp.float32)
    limits = pltpu.CompilerParams(vmem_limit_bytes=32 * 1024 * 1024)

    def exchange(pieces):
        return [
            lax.ppermute(pieces[d], "path", [(i, i ^ d) for i in range(paths)])
            for d in range(1, paths)
        ]

    places, *packed = pl.pallas_call(
        functools.partial(pack_kernel, paths, owned),
        out_shape=[jax.ShapeDtypeStruct((slots,), jnp.int32)] + [piece] * paths,
        in_specs=[SMEM, SMEM, ANY],
        out_specs=[SMEM] + [ANY] * paths,
        scratch_shapes=[pltpu.SMEM((paths,), jnp.int32), pltpu.SemaphoreType.DMA((slots,))],
        name="pack",
    )(me, module_ids, path_params.reshape(held, rows, width))
    arrived = exchange(packed)
    table, weights, total, acc, base = pl.pallas_call(
        functools.partial(early_kernel, paths),
        out_shape=[
            jax.ShapeDtypeStruct((slots,), jnp.int32),
            jax.ShapeDtypeStruct((slots,), jnp.float32),
            jax.ShapeDtypeStruct((owned,), jnp.float32),
            pltpu.VMEM(module.shape, module.dtype),
            pltpu.VMEM(module.shape, module.dtype),
        ],
        in_specs=[SMEM] * 3 + [VMEM] * 3,
        out_specs=[SMEM] * 3 + [VMEM] * 2,
        compiler_params=limits,
        cost_estimate=pl.CostEstimate(flops=10**6, bytes_accessed=12 * 2**20, transcendentals=0),
        name="early",
    )(me, module_ids, counts, packed[0], global_params, momentum)
    acc, squares = pl.pallas_call(
        functools.partial(combine_kernel, paths),
        out_shape=[
            pltpu.VMEM(module.shape, module.dtype),
            jax.ShapeDtypeStruct((owned, 128), jnp.float32),
        ],
        in_specs=[SMEM] * 4 + [VMEM] * paths,
        out_specs=[VMEM] * 2,
        input_output_aliases={4: 0},
        compiler_params=limits,
        name="combine",
    )(me, table, weights, total, in_vmem(acc), *arrived)
    parts = [squares] + [
        lax.ppermute(squares, "shard", [(i, (i + d) % shards) for i in range(shards)])
        for d in range(1, shards)
    ]
    scale, *outgoing = pl.pallas_call(
        functools.partial(send_kernel, paths, shards),
        out_shape=[jax.ShapeDtypeStruct((owned, rows, 128), jnp.float32)] + [piece] * paths,
        in_specs=[SMEM] * 3 + [VMEM] * (2 + shards),
        out_specs=[VMEM] * (1 + paths),
        compiler_params=limits,
        name="send",
    )(me, table, total, in_vmem(acc), in_vmem(base), *parts)
    returned = exchange(outgoing)
    block = pl.BlockSpec((1, rows, width), lambda m: (m, 0, 0))
    updated, velocity = pl.pallas_call(
        store_kernel,
        out_shape=[module] * 2,
        grid=(owned,),
        in_specs=[pl.BlockSpec((1, rows, 128), lambda m: (m, 0, 0))] + [block] * 3,
        out_specs=[block] * 2,
        compiler_params=limits,
        cost_estimate=pl.CostEstimate(flops=10**6, bytes_accessed=12 * 2**20, transcendentals=0),
        name="store",
    )(scale, acc, base, momentum)
    path_out = pl.pallas_call(
        functools.partial(unpack_kernel, paths),
        out_shape=jax.ShapeDtypeStruct(path_params.shape, path_params.dtype),
        in_specs=[SMEM] * 2 + [ANY] * paths,
        out_specs=ANY,
        scratch_shapes=[pltpu.SemaphoreType.DMA((slots,))],
        name="unpack",
    )(me, places, outgoing[0], *returned)
    return updated, velocity, path_out


def solution(mesh):
    placed = (
        P("path", None, "shard", None),
        P("path", "shard", None),
        P("path", "shard", None),
        P(),
        P(),
    )
    return jax.shard_map(
        on_device,
        mesh=mesh,
        in_specs=placed,
        out_specs=(
            P("path", "shard", None),
            P("path", "shard", None),
            P("path", None, "shard", None),
        ),
        check_vma=False,
    )
```

```python
import functools

import jax
import jax.numpy as jnp
from jax import lax
from jax.experimental import pallas as pl
from jax.experimental.pallas import tpu as pltpu
from jax.sharding import PartitionSpec as P

CAP = 2
CHUNK = 1024
PARTS = 4
outer_momentum = 0.9
outer_rate = 0.7

SMEM = pl.BlockSpec(memory_space=pltpu.SMEM)
VMEM = pl.BlockSpec(memory_space=pltpu.VMEM)
ANY = pl.BlockSpec(memory_space=pl.ANY)


def in_vmem(x):
    return pltpu.with_memory_space_constraint(x, pltpu.VMEM)


def chunks(width):
    step = CHUNK if width % CHUNK == 0 else width
    return [pl.ds(at, step) for at in range(0, width, step)]


def pack_kernel(paths, owned, me_ref, ids_ref, local_ref, places_ref, *rest):
    pieces, (seen, sems) = rest[:paths], rest[paths:]
    me = me_ref[0]
    held = ids_ref.shape[1]

    def clear(i, _):
        places_ref[i] = jnp.int32(-1)
        return 0

    def reset(i, _):
        seen[i] = jnp.int32(0)
        return 0

    def place(k, _):
        group = ids_ref[me, k] // owned
        rank = seen[group]
        seen[group] = rank + 1
        places_ref[group * CAP + rank] = k
        return 0

    lax.fori_loop(0, paths * CAP, clear, 0)
    lax.fori_loop(0, paths, reset, 0)
    lax.fori_loop(0, held, place, 0)
    copies = []
    for d in list(range(1, paths)) + [0]:
        for r in range(CAP):
            k = jnp.maximum(places_ref[(me ^ d) * CAP + r], 0)
            copy = pltpu.make_async_copy(
                local_ref.at[k], pieces[d].at[r], sems.at[d * CAP + r]
            )
            copy.start()
            copies.append(copy)
    for copy in copies:
        copy.wait()


def early_kernel(
    paths, me_ref, ids_ref, counts_ref, own_ref, params_hbm, past_hbm,
    module_ref, weight_ref, total_ref, acc_ref, base_ref, params_ref, past_ref, sems,
):
    me = me_ref[0]
    owned, _, width = acc_ref.shape
    held = ids_ref.shape[1]
    part = owned // PARTS

    def copies(i):
        at = pl.ds(i * part, part)
        return [
            pltpu.make_async_copy(hbm.at[at], ref.at[at], sems.at[n, i])
            for n, (hbm, ref) in enumerate(((params_hbm, params_ref), (past_hbm, past_ref)))
        ]

    for i in range(PARTS):
        for copy in copies(i):
            copy.start()

    def reset(i, _):
        total_ref[i] = jnp.float32(0.0)
        return 0

    def one(path, _):
        first = path * (CAP + 1)
        for r in range(CAP):
            module_ref[first + r] = jnp.int32(0)
            weight_ref[first + r] = jnp.float32(0.0)
        rank = jnp.int32(0)
        for k in range(held):
            at = ids_ref[path, k] - me * owned
            mine = (at >= 0) & (at < owned)
            slot = first + jnp.where(mine, rank, CAP)
            module_ref[slot] = at
            weight_ref[slot] = counts_ref[path, k]
            rank = rank + mine.astype(jnp.int32)
        for r in range(CAP):
            at = module_ref[first + r]
            total_ref[at] = total_ref[at] + weight_ref[first + r]
        return 0

    lax.fori_loop(0, owned, reset, 0)
    lax.fori_loop(0, paths, one, 0)
    for i in range(PARTS):
        for copy in copies(i):
            copy.wait()

        def fill(m, _):
            for c in chunks(width):
                params = params_ref[m, :, c]
                acc_ref[m, :, c] = total_ref[m] * params
                base_ref[m, :, c] = params - (outer_rate * outer_momentum**2) * past_ref[m, :, c]
            return 0

        lax.fori_loop(i * part, (i + 1) * part, fill, 0)
    subtract(me, [own_ref], [0], module_ref, weight_ref, acc_ref)


def subtract(me, pieces, distances, module_ref, weight_ref, acc_ref):
    width = acc_ref.shape[2]
    for piece, d in zip(pieces, distances, strict=True):
        for r in range(CAP):
            slot = (me ^ d) * (CAP + 1) + r
            m, weight = module_ref[slot], weight_ref[slot]
            for c in chunks(width):
                acc_ref[m, :, c] = acc_ref[m, :, c] - weight * piece[r, :, c].astype(jnp.float32)


def combine_kernel(paths, me_ref, module_ref, weight_ref, total_ref, acc_in, *rest):
    pieces, (acc_ref, squares_ref) = rest[: paths - 1], rest[paths - 1 :]
    subtract(me_ref[0], pieces, range(1, paths), module_ref, weight_ref, acc_ref)
    owned, rows, width = acc_ref.shape
    for m in range(owned):
        inverse = 1.0 / jnp.maximum(jnp.full((rows, 128), total_ref[m], jnp.float32), 1.0)
        added = jnp.zeros((rows, 128), jnp.float32)
        for at in range(0, width, 128):
            raw = acc_ref[m, :, pl.ds(at, 128)] * inverse
            added = added + raw * raw
        squares_ref[pl.ds(m, 1), :] = jnp.sum(added, axis=0, keepdims=True)


def scales(entries, total, squares):
    inverse = 1.0 / jnp.maximum(total, 1.0)
    mean = jnp.sum(squares, axis=1, keepdims=True) / entries
    factor = jnp.minimum(1.0, 1.0 / jnp.sqrt(mean + 1e-06))
    return inverse * factor


def send_kernel(paths, shards, me_ref, module_ref, total_ref, acc_ref, base_ref, *rest):
    squares, (scale_ref, *pieces) = rest[:shards], rest[shards:]
    me = me_ref[0]
    owned, rows, width = acc_ref.shape
    summed = squares[0][...]
    for other in squares[1:]:
        summed = summed + other[...]
    total = jnp.concatenate(
        [jnp.full((1, 128), total_ref[m], jnp.float32) for m in range(owned)], axis=0
    )
    scale = scales(rows * width * shards, total, summed)
    for m in range(owned):
        scale_ref[m] = jnp.broadcast_to(scale[m : m + 1, :], (rows, 128))
    rate = outer_rate * (1.0 + outer_momentum)
    for d in list(range(1, paths)) + [0]:
        for r in range(CAP):
            m = module_ref[(me ^ d) * (CAP + 1) + r]
            step = rate * scale_ref[m][:, :1]
            for c in chunks(width):
                pieces[d][r, :, c] = (base_ref[m, :, c] - step * acc_ref[m, :, c]).astype(
                    jnp.bfloat16
                )


def store_kernel(scale_ref, acc_ref, base_ref, past_ref, updated_ref, velocity_ref):
    rate = outer_rate * (1.0 + outer_momentum)
    scale = scale_ref[0][:, :1]
    for c in chunks(acc_ref.shape[2]):
        delta = scale * acc_ref[0, :, c]
        updated_ref[0, :, c] = base_ref[0, :, c] - rate * delta
        velocity_ref[0, :, c] = outer_momentum * past_ref[0, :, c] + delta


def unpack_kernel(paths, me_ref, places_ref, *rest):
    pieces, (out_ref, sems) = rest[:paths], rest[paths:]
    me = me_ref[0]
    for wait in (False, True):
        for d in range(paths):
            for r in range(CAP):
                k = places_ref[(me ^ d) * CAP + r]

                @pl.when(k >= 0)
                def _():
                    copy = pltpu.make_async_copy(
                        pieces[d].at[r], out_ref.at[0, k], sems.at[d * CAP + r]
                    )
                    if wait:
                        copy.wait()
                    else:
                        copy.start()


def on_device(path_params, global_params, momentum, module_ids, token_counts):
    paths, held = module_ids.shape
    owned, rows, width = global_params.shape
    shards = lax.axis_size("shard")
    me = lax.axis_index("path").astype(jnp.int32).reshape(1)
    counts = token_counts.astype(jnp.float32)
    slots = paths * CAP
    piece = pltpu.VMEM((CAP, rows, width), jnp.bfloat16)
    module = jax.ShapeDtypeStruct((owned, rows, width), jnp.float32)
    limits = pltpu.CompilerParams(vmem_limit_bytes=32 * 1024 * 1024)

    def exchange(pieces):
        return [
            lax.ppermute(pieces[d], "path", [(i, i ^ d) for i in range(paths)])
            for d in range(1, paths)
        ]

    places, *packed = pl.pallas_call(
        functools.partial(pack_kernel, paths, owned),
        out_shape=[jax.ShapeDtypeStruct((slots,), jnp.int32)] + [piece] * paths,
        in_specs=[SMEM, SMEM, ANY],
        out_specs=[SMEM] + [VMEM] * paths,
        scratch_shapes=[pltpu.SMEM((paths,), jnp.int32), pltpu.SemaphoreType.DMA((slots,))],
        name="pack",
    )(me, module_ids, path_params.reshape(held, rows, width))
    arrived = exchange(packed)
    table, weights, total, acc, base = pl.pallas_call(
        functools.partial(early_kernel, paths),
        out_shape=[
            jax.ShapeDtypeStruct((paths * (CAP + 1),), jnp.int32),
            jax.ShapeDtypeStruct((paths * (CAP + 1),), jnp.float32),
            jax.ShapeDtypeStruct((owned,), jnp.float32),
            pltpu.VMEM(module.shape, module.dtype),
            pltpu.VMEM(module.shape, module.dtype),
        ],
        in_specs=[SMEM] * 3 + [VMEM] + [ANY] * 2,
        out_specs=[SMEM] * 3 + [VMEM] * 2,
        scratch_shapes=[
            pltpu.VMEM(module.shape, module.dtype),
            pltpu.VMEM(module.shape, module.dtype),
            pltpu.SemaphoreType.DMA((2, PARTS)),
        ],
        compiler_params=limits,
        cost_estimate=pl.CostEstimate(flops=10**6, bytes_accessed=12 * 2**20, transcendentals=0),
        name="early",
    )(me, module_ids, counts, in_vmem(packed[0]), global_params, momentum)
    acc, squares = pl.pallas_call(
        functools.partial(combine_kernel, paths),
        out_shape=[
            pltpu.VMEM(module.shape, module.dtype),
            jax.ShapeDtypeStruct((owned, 128), jnp.float32),
        ],
        in_specs=[SMEM] * 4 + [VMEM] * paths,
        out_specs=[VMEM] * 2,
        input_output_aliases={4: 0},
        compiler_params=limits,
        name="combine",
    )(me, table, weights, total, in_vmem(acc), *[in_vmem(x) for x in arrived])
    parts = [squares] + [
        lax.ppermute(squares, "shard", [(i, (i + d) % shards) for i in range(shards)])
        for d in sorted(range(1, shards), key=lambda d: (d != 2, d))
    ]
    scale, *outgoing = pl.pallas_call(
        functools.partial(send_kernel, paths, shards),
        out_shape=[jax.ShapeDtypeStruct((owned, rows, 128), jnp.float32)] + [piece] * paths,
        in_specs=[SMEM] * 3 + [VMEM] * (2 + shards),
        out_specs=[VMEM] * (1 + paths),
        compiler_params=limits,
        name="send",
    )(me, table, total, in_vmem(acc), in_vmem(base), *parts)
    returned = exchange(outgoing)
    block = pl.BlockSpec((1, rows, width), lambda m: (m, 0, 0))
    updated, velocity = pl.pallas_call(
        store_kernel,
        out_shape=[module] * 2,
        grid=(owned,),
        in_specs=[pl.BlockSpec((1, rows, 128), lambda m: (m, 0, 0))] + [block] * 3,
        out_specs=[block] * 2,
        compiler_params=limits,
        cost_estimate=pl.CostEstimate(flops=10**6, bytes_accessed=12 * 2**20, transcendentals=0),
        name="store",
    )(scale, acc, base, momentum)
    path_out = pl.pallas_call(
        functools.partial(unpack_kernel, paths),
        out_shape=jax.ShapeDtypeStruct(path_params.shape, path_params.dtype),
        in_specs=[SMEM] * 2 + [VMEM] * paths,
        out_specs=ANY,
        scratch_shapes=[pltpu.SemaphoreType.DMA((slots,))],
        name="unpack",
    )(me, places, *[in_vmem(x) for x in [outgoing[0], *returned]])
    return updated, velocity, path_out


def solution(mesh):
    placed = (
        P("path", None, "shard", None),
        P("path", "shard", None),
        P("path", "shard", None),
        P(),
        P(),
    )
    return jax.shard_map(
        on_device,
        mesh=mesh,
        in_specs=placed,
        out_specs=(
            P("path", "shard", None),
            P("path", "shard", None),
            P("path", None, "shard", None),
        ),
        check_vma=False,
    )
```

```python
import functools

import jax
import jax.numpy as jnp
from jax import lax
from jax.experimental import pallas as pl
from jax.experimental.pallas import tpu as pltpu
from jax.sharding import PartitionSpec as P

CAP = 2
CHUNK = 1024
PARTS = 4
outer_momentum = 0.9
outer_rate = 0.7

SMEM = pl.BlockSpec(memory_space=pltpu.SMEM)
VMEM = pl.BlockSpec(memory_space=pltpu.VMEM)
ANY = pl.BlockSpec(memory_space=pl.ANY)


def in_vmem(*arrays):
    return [pltpu.with_memory_space_constraint(x, pltpu.VMEM) for x in arrays]


def in_hbm(*arrays):
    return [pltpu.with_memory_space_constraint(x, pltpu.HBM) for x in arrays]


def chunks(width):
    step = CHUNK if width % CHUNK == 0 else width
    return [pl.ds(at, step) for at in range(0, width, step)]


def pack_kernel(paths, owned, order, me_ref, ids_ref, local_ref, places_ref, *rest):
    pieces, (seen, sems) = rest[:paths], rest[paths:]
    me = me_ref[0]
    for i in range(paths):
        seen[i] = jnp.int32(0)
    for i in range(paths * CAP):
        places_ref[i] = jnp.int32(-1)
    for k in range(ids_ref.shape[1]):
        group = lax.div(ids_ref[me, k], jnp.int32(owned))
        rank = seen[group]
        seen[group] = rank + 1
        places_ref[group * CAP + rank] = jnp.int32(k)
    copies = []
    for d in order:
        for r in range(CAP):
            k = jnp.maximum(places_ref[(me ^ d) * CAP + r], 0)
            copy = pltpu.make_async_copy(
                local_ref.at[k], pieces[d].at[r], sems.at[d * CAP + r]
            )
            copy.start()
            copies.append(copy)
    for copy in copies:
        copy.wait()


def find_slots(me, owned, ids_ref, counts_ref, module_ref, weight_ref, total_ref):
    paths, held = ids_ref.shape

    def reset(i, _):
        total_ref[i] = jnp.float32(0.0)
        return 0

    def one(path, _):
        first = path * (CAP + 1)
        for r in range(CAP):
            module_ref[first + r] = jnp.int32(0)
            weight_ref[first + r] = jnp.float32(0.0)
        rank = jnp.int32(0)
        for k in range(held):
            at = ids_ref[path, k] - me * owned
            mine = (at >= 0) & (at < owned)
            slot = first + jnp.where(mine, rank, CAP)
            module_ref[slot] = at
            weight_ref[slot] = counts_ref[path, k].astype(jnp.float32)
            rank = rank + mine.astype(jnp.int32)
        for r in range(CAP):
            at = module_ref[first + r]
            total_ref[at] = total_ref[at] + weight_ref[first + r]
        return 0

    lax.fori_loop(0, owned, reset, 0)
    lax.fori_loop(0, paths, one, 0)


def subtract(me, pieces, distances, module_ref, weight_ref, acc_ref):
    width = acc_ref.shape[2]
    for piece, d in zip(pieces, distances, strict=True):
        for r in range(CAP):
            slot = (me ^ d) * (CAP + 1) + r
            m, weight = module_ref[slot], weight_ref[slot]
            for c in chunks(width):
                acc_ref[m, :, c] = acc_ref[m, :, c] - weight * piece[r, :, c].astype(jnp.float32)


def prepare(me, own_ref, params_hbm, past_hbm, tables, acc_ref, base_ref, params_ref, past_ref, sems, find):
    owned, _, width = acc_ref.shape
    part = owned // PARTS

    def copies(i):
        at = pl.ds(i * part, part)
        return [
            pltpu.make_async_copy(hbm.at[at], ref.at[at], sems.at[n, i])
            for n, (hbm, ref) in enumerate(((params_hbm, params_ref), (past_hbm, past_ref)))
        ]

    for i in range(PARTS):
        for copy in copies(i):
            copy.start()
    find()
    module_ref, weight_ref, total_ref = tables
    for i in range(PARTS):
        for copy in copies(i):
            copy.wait()

        def fill(m, _):
            for c in chunks(width):
                params = params_ref[m, :, c]
                acc_ref[m, :, c] = total_ref[m] * params
                base_ref[m, :, c] = params - (outer_rate * outer_momentum**2) * past_ref[m, :, c]
            return 0

        lax.fori_loop(i * part, (i + 1) * part, fill, 0)
    subtract(me, [own_ref], [0], module_ref, weight_ref, acc_ref)


def before_kernel(me_ref, ids_ref, counts_ref, own_ref, params_hbm, past_hbm, *rest):
    acc_ref, base_ref, *_, module_ref, weight_ref, total_ref, params_ref, past_ref, sems = rest[
        (len(rest) - 8) // 2 :
    ]
    me = me_ref[0]
    tables = module_ref, weight_ref, total_ref

    @pl.when(lax.rem(me, 2) == 1)
    def _():
        find = functools.partial(find_slots, me, acc_ref.shape[0], ids_ref, counts_ref, *tables)
        prepare(
            me, own_ref, params_hbm, past_hbm, tables, acc_ref, base_ref, params_ref, past_ref, sems, find
        )


def beside_kernel(
    me_ref, ids_ref, counts_ref, own_ref, params_hbm, past_hbm, _acc, _base,
    module_ref, weight_ref, total_ref, acc_ref, base_ref, params_ref, past_ref, sems,
):
    me = me_ref[0]
    tables = module_ref, weight_ref, total_ref
    find = functools.partial(find_slots, me, acc_ref.shape[0], ids_ref, counts_ref, *tables)

    @pl.when(lax.rem(me, 2) == 1)
    def _():
        find()

    @pl.when(lax.rem(me, 2) == 0)
    def _():
        prepare(
            me, own_ref, params_hbm, past_hbm, tables, acc_ref, base_ref, params_ref, past_ref, sems, find
        )


def combine_kernel(paths, me_ref, module_ref, weight_ref, total_ref, acc_in, *rest):
    pieces, (acc_ref, squares_ref) = rest[: paths - 1], rest[paths - 1 :]
    subtract(me_ref[0], pieces, range(1, paths), module_ref, weight_ref, acc_ref)
    owned, rows, width = acc_ref.shape
    for m in range(owned):
        inverse = 1.0 / jnp.maximum(jnp.full((rows, 128), total_ref[m], jnp.float32), 1.0)
        added = jnp.zeros((rows, 128), jnp.float32)
        for at in range(0, width, 128):
            raw = acc_ref[m, :, pl.ds(at, 128)] * inverse
            added = added + raw * raw
        squares_ref[pl.ds(m, 1), :] = jnp.sum(added, axis=0, keepdims=True)


def scales(entries, total, squares):
    inverse = 1.0 / jnp.maximum(total, 1.0)
    mean = jnp.sum(squares, axis=1, keepdims=True) / entries
    factor = jnp.minimum(1.0, 1.0 / jnp.sqrt(mean + 1e-06))
    return inverse * factor


def send_kernel(paths, shards, me_ref, module_ref, total_ref, acc_ref, base_ref, *rest):
    squares, (scale_ref, *pieces) = rest[:shards], rest[shards:]
    me = me_ref[0]
    owned, rows, width = acc_ref.shape
    summed = squares[0][...]
    for other in squares[1:]:
        summed = summed + other[...]
    total = jnp.concatenate(
        [jnp.full((1, 128), total_ref[m], jnp.float32) for m in range(owned)], axis=0
    )
    scale = scales(rows * width * shards, total, summed)
    for m in range(owned):
        scale_ref[m] = jnp.broadcast_to(scale[m : m + 1, :], (rows, 128))
    rate = outer_rate * (1.0 + outer_momentum)
    for d in range(paths):
        for r in range(CAP):
            m = module_ref[(me ^ d) * (CAP + 1) + r]
            step = rate * scale_ref[m][:, :1]
            for c in chunks(width):
                pieces[d][r, :, c] = (base_ref[m, :, c] - step * acc_ref[m, :, c]).astype(
                    jnp.bfloat16
                )


def store_kernel(
    scale_ref, acc_ref, base_ref, past_ref, updated_hbm, velocity_hbm, updated_ref, velocity_ref, sems
):
    rate = outer_rate * (1.0 + outer_momentum)
    owned, _, width = acc_ref.shape
    part = owned // PARTS

    def copies(i):
        at = pl.ds(i * part, part)
        return [
            pltpu.make_async_copy(ref.at[at], hbm.at[at], sems.at[n, i])
            for n, (ref, hbm) in enumerate(
                ((updated_ref, updated_hbm), (velocity_ref, velocity_hbm))
            )
        ]

    for i in range(PARTS):

        def fill(m, _):
            scale = scale_ref[m][:, :1]
            for c in chunks(width):
                delta = scale * acc_ref[m, :, c]
                updated_ref[m, :, c] = base_ref[m, :, c] - rate * delta
                velocity_ref[m, :, c] = outer_momentum * past_ref[m, :, c] + delta
            return 0

        lax.fori_loop(i * part, (i + 1) * part, fill, 0)
        for copy in copies(i):
            copy.start()
    for i in range(PARTS):
        for copy in copies(i):
            copy.wait()


def unpack_kernel(paths, me_ref, places_ref, *rest):
    pieces, (out_ref, sems) = rest[:paths], rest[paths:]
    me = me_ref[0]
    for wait in (False, True):
        for d in range(paths):
            for r in range(CAP):
                k = places_ref[(me ^ d) * CAP + r]

                @pl.when(k >= 0)
                def _():
                    copy = pltpu.make_async_copy(
                        pieces[d].at[r], out_ref.at[0, k], sems.at[d * CAP + r]
                    )
                    if wait:
                        copy.wait()
                    else:
                        copy.start()


def on_device(path_params, global_params, momentum, module_ids, token_counts):
    paths, held = module_ids.shape
    owned, rows, width = global_params.shape
    shards = lax.axis_size("shard")
    me = lax.axis_index("path").astype(jnp.int32).reshape(1)
    module_ids, counts = in_hbm(module_ids, token_counts)
    slots = paths * CAP
    piece = pltpu.VMEM((CAP, rows, width), jnp.bfloat16)
    module = jax.ShapeDtypeStruct((owned, rows, width), jnp.float32)
    held_module = pltpu.VMEM(module.shape, module.dtype)
    tables = [
        jax.ShapeDtypeStruct((paths * (CAP + 1),), jnp.int32),
        jax.ShapeDtypeStruct((paths * (CAP + 1),), jnp.float32),
        jax.ShapeDtypeStruct((owned,), jnp.float32),
    ]
    room = [
        pltpu.VMEM(module.shape, module.dtype),
        pltpu.VMEM(module.shape, module.dtype),
        pltpu.SemaphoreType.DMA((2, PARTS)),
    ]
    limits = pltpu.CompilerParams(vmem_limit_bytes=24 * 1024 * 1024)
    far = sorted(range(2, paths, 2), key=lambda d: (-d.bit_count(), d))

    def to(x, d):
        return lax.ppermute(x, "path", [(i, i ^ d) for i in range(paths)])

    order = [d ^ 1 for d in far] + far + [1, 0]
    places, *packed = pl.pallas_call(
        functools.partial(pack_kernel, paths, owned, order),
        out_shape=[jax.ShapeDtypeStruct((slots,), jnp.int32)] + [piece] * paths,
        in_specs=[SMEM, SMEM, ANY],
        out_specs=[SMEM] + [VMEM] * paths,
        scratch_shapes=[pltpu.SMEM((paths,), jnp.int32), pltpu.SemaphoreType.DMA((slots,))],
        name="pack",
    )(me, module_ids, *in_hbm(path_params.reshape(held, rows, width)))

    through = [packed[d] for d in far] + [to(packed[d ^ 1], 1) for d in far]
    fixed = 6
    acc, base, *passed = pl.pallas_call(
        before_kernel,
        out_shape=[held_module] * 2 + [piece] * len(through),
        in_specs=[SMEM] * 3 + [VMEM] + [ANY] * 2 + [VMEM] * len(through),
        out_specs=[VMEM] * (2 + len(through)),
        input_output_aliases={fixed + i: 2 + i for i in range(len(through))},
        scratch_shapes=[
            pltpu.SMEM(tables[0].shape, jnp.int32),
            pltpu.SMEM(tables[1].shape, jnp.float32),
            pltpu.SMEM(tables[2].shape, jnp.float32),
        ]
        + room,
        compiler_params=limits,
        name="before",
    )(
        me, module_ids, counts, *in_vmem(packed[0]), *in_hbm(global_params, momentum),
        *in_vmem(*through),
    )
    arrived = {}
    for d, x in zip(far, passed[: len(far)], strict=True):
        arrived[d] = to(x, d)
    for d, x in zip(far, passed[len(far) :], strict=True):
        arrived[d ^ 1] = to(x, d)
    arrived[1] = to(packed[1], 1)
    table, weights, total, acc, base = pl.pallas_call(
        beside_kernel,
        out_shape=tables + [held_module] * 2,
        in_specs=[SMEM] * 3 + [VMEM] + [ANY] * 2 + [VMEM] * 2,
        out_specs=[SMEM] * 3 + [VMEM] * 2,
        input_output_aliases={fixed: 3, fixed + 1: 4},
        scratch_shapes=room,
        compiler_params=limits,
        cost_estimate=pl.CostEstimate(flops=10**6, bytes_accessed=12 * 2**20, transcendentals=0),
        name="beside",
    )(
        me, module_ids, counts, *in_vmem(packed[0]), *in_hbm(global_params, momentum),
        *in_vmem(acc, base),
    )
    acc, squares = pl.pallas_call(
        functools.partial(combine_kernel, paths),
        out_shape=[held_module, jax.ShapeDtypeStruct((owned, 128), jnp.float32)],
        in_specs=[SMEM] * 4 + [VMEM] * paths,
        out_specs=[VMEM] * 2,
        input_output_aliases={4: 0},
        compiler_params=limits,
        name="combine",
    )(me, table, weights, total, *in_vmem(acc, *[arrived[d] for d in range(1, paths)]))
    parts = [squares] + [
        lax.ppermute(squares, "shard", [(i, (i + d) % shards) for i in range(shards)])
        for d in sorted(range(1, shards), key=lambda d: (d != 2, d))
    ]
    scale, *outgoing = pl.pallas_call(
        functools.partial(send_kernel, paths, shards),
        out_shape=[jax.ShapeDtypeStruct((owned, rows, 128), jnp.float32)] + [piece] * paths,
        in_specs=[SMEM] * 3 + [VMEM] * (2 + shards),
        out_specs=[VMEM] * (1 + paths),
        compiler_params=limits,
        name="send",
    )(me, table, total, *in_vmem(acc, base), *parts)
    relayed = {d: to(outgoing[d ^ 1], d) for d in far}
    returned = {0: outgoing[0]}
    for d in far:
        returned[d] = to(outgoing[d], d)
    returned[1] = to(outgoing[1], 1)
    for d in far:
        returned[d ^ 1] = to(relayed[d], 1)
    updated, velocity = pl.pallas_call(
        store_kernel,
        out_shape=[module] * 2,
        in_specs=[VMEM] * 4,
        out_specs=[ANY] * 2,
        scratch_shapes=room,
        compiler_params=limits,
        cost_estimate=pl.CostEstimate(flops=10**6, bytes_accessed=12 * 2**20, transcendentals=0),
        name="store",
    )(scale, *in_vmem(acc, base), momentum)
    path_out = pl.pallas_call(
        functools.partial(unpack_kernel, paths),
        out_shape=jax.ShapeDtypeStruct(path_params.shape, path_params.dtype),
        in_specs=[SMEM] * 2 + [VMEM] * paths,
        out_specs=ANY,
        scratch_shapes=[pltpu.SemaphoreType.DMA((slots,))],
        name="unpack",
    )(me, places, *in_vmem(*[returned[d] for d in range(paths)]))
    return updated, velocity, path_out


def solution(mesh):
    placed = (
        P("path", None, "shard", None),
        P("path", "shard", None),
        P("path", "shard", None),
        P(),
        P(),
    )
    return jax.shard_map(
        on_device,
        mesh=mesh,
        in_specs=placed,
        out_specs=(
            P("path", "shard", None),
            P("path", "shard", None),
            P("path", None, "shard", None),
        ),
        check_vma=False,
    )
```

```python
import functools

import jax
import jax.numpy as jnp
from jax import lax
from jax.experimental import pallas as pl
from jax.experimental.pallas import tpu as pltpu
from jax.sharding import PartitionSpec as P

CAP = 2
CHUNK = 1024
PARTS = 4
outer_momentum = 0.9
outer_rate = 0.7

SMEM = pl.BlockSpec(memory_space=pltpu.SMEM)
VMEM = pl.BlockSpec(memory_space=pltpu.VMEM)
ANY = pl.BlockSpec(memory_space=pl.ANY)


def in_vmem(*arrays):
    return [pltpu.with_memory_space_constraint(x, pltpu.VMEM) for x in arrays]


def in_hbm(*arrays):
    return [pltpu.with_memory_space_constraint(x, pltpu.HBM) for x in arrays]


def chunks(width):
    step = CHUNK if width % CHUNK == 0 else width
    return [pl.ds(at, step) for at in range(0, width, step)]


def pack_kernel(paths, owned, order, me_ref, ids_ref, local_ref, places_ref, *rest):
    pieces, (seen, sems) = rest[:paths], rest[paths:]
    me = me_ref[0]
    for i in range(paths):
        seen[i] = jnp.int32(0)
    for i in range(paths * CAP):
        places_ref[i] = jnp.int32(-1)
    for k in range(ids_ref.shape[1]):
        group = lax.div(ids_ref[me, k], jnp.int32(owned))
        rank = seen[group]
        seen[group] = rank + 1
        places_ref[group * CAP + rank] = jnp.int32(k)
    copies = []
    for d in order:
        for r in range(CAP):
            k = jnp.maximum(places_ref[(me ^ d) * CAP + r], 0)
            copy = pltpu.make_async_copy(
                local_ref.at[k], pieces[d].at[r], sems.at[d * CAP + r]
            )
            copy.start()
            copies.append(copy)
    for copy in copies:
        copy.wait()


def find_slots(me, owned, ids_ref, counts_ref, module_ref, weight_ref, total_ref):
    paths, held = ids_ref.shape

    def reset(i, _):
        total_ref[i] = jnp.float32(0.0)
        return 0

    def one(path, _):
        first = path * (CAP + 1)
        for r in range(CAP):
            module_ref[first + r] = jnp.int32(0)
            weight_ref[first + r] = jnp.float32(0.0)
        rank = jnp.int32(0)
        for k in range(held):
            at = ids_ref[path, k] - me * owned
            mine = (at >= 0) & (at < owned)
            slot = first + jnp.where(mine, rank, CAP)
            module_ref[slot] = at
            weight_ref[slot] = counts_ref[path, k].astype(jnp.float32)
            rank = rank + mine.astype(jnp.int32)
        for r in range(CAP):
            at = module_ref[first + r]
            total_ref[at] = total_ref[at] + weight_ref[first + r]
        return 0

    lax.fori_loop(0, owned, reset, 0)
    lax.fori_loop(0, paths, one, 0)


def subtract(me, pieces, distances, module_ref, weight_ref, acc_ref):
    width = acc_ref.shape[2]
    for piece, d in zip(pieces, distances, strict=True):
        for r in range(CAP):
            slot = (me ^ d) * (CAP + 1) + r
            m, weight = module_ref[slot], weight_ref[slot]
            for c in chunks(width):
                acc_ref[m, :, c] = acc_ref[m, :, c] - weight * piece[r, :, c].astype(jnp.float32)


def prepare(me, own_ref, params_hbm, past_hbm, tables, acc_ref, base_ref, params_ref, past_ref, sems, find):
    owned, _, width = acc_ref.shape
    part = owned // PARTS

    def copies(i):
        at = pl.ds(i * part, part)
        return [
            pltpu.make_async_copy(hbm.at[at], ref.at[at], sems.at[n, i])
            for n, (hbm, ref) in enumerate(((params_hbm, params_ref), (past_hbm, past_ref)))
        ]

    for i in range(PARTS):
        for copy in copies(i):
            copy.start()
    find()
    module_ref, weight_ref, total_ref = tables
    for i in range(PARTS):
        for copy in copies(i):
            copy.wait()

        def fill(m, _):
            for c in chunks(width):
                params = params_ref[m, :, c]
                acc_ref[m, :, c] = total_ref[m] * params
                base_ref[m, :, c] = params - (outer_rate * outer_momentum**2) * past_ref[m, :, c]
            return 0

        lax.fori_loop(i * part, (i + 1) * part, fill, 0)
    subtract(me, [own_ref], [0], module_ref, weight_ref, acc_ref)


def early_kernel(
    me_ref, ids_ref, counts_ref, own_ref, params_hbm, past_hbm,
    module_ref, weight_ref, total_ref, acc_ref, base_ref, params_ref, past_ref, sems,
):
    me = me_ref[0]
    tables = module_ref, weight_ref, total_ref
    find = functools.partial(find_slots, me, acc_ref.shape[0], ids_ref, counts_ref, *tables)
    prepare(
        me, own_ref, params_hbm, past_hbm, tables, acc_ref, base_ref, params_ref, past_ref, sems, find
    )


def combine_kernel(paths, me_ref, module_ref, weight_ref, total_ref, acc_in, *rest):
    pieces, (acc_ref, squares_ref) = rest[: paths - 1], rest[paths - 1 :]
    subtract(me_ref[0], pieces, range(1, paths), module_ref, weight_ref, acc_ref)
    owned, rows, width = acc_ref.shape
    for m in range(owned):
        inverse = 1.0 / jnp.maximum(jnp.full((rows, 128), total_ref[m], jnp.float32), 1.0)
        added = jnp.zeros((rows, 128), jnp.float32)
        for at in range(0, width, 128):
            raw = acc_ref[m, :, pl.ds(at, 128)] * inverse
            added = added + raw * raw
        squares_ref[pl.ds(m, 1), :] = jnp.sum(added, axis=0, keepdims=True)


def scales(entries, total, squares):
    inverse = 1.0 / jnp.maximum(total, 1.0)
    mean = jnp.sum(squares, axis=1, keepdims=True) / entries
    factor = jnp.minimum(1.0, 1.0 / jnp.sqrt(mean + 1e-06))
    return inverse * factor


def send_kernel(paths, shards, me_ref, module_ref, total_ref, acc_ref, base_ref, *rest):
    squares, (scale_ref, *pieces) = rest[:shards], rest[shards:]
    me = me_ref[0]
    owned, rows, width = acc_ref.shape
    summed = squares[0][...]
    for other in squares[1:]:
        summed = summed + other[...]
    total = jnp.concatenate(
        [jnp.full((1, 128), total_ref[m], jnp.float32) for m in range(owned)], axis=0
    )
    scale = scales(rows * width * shards, total, summed)
    for m in range(owned):
        scale_ref[m] = jnp.broadcast_to(scale[m : m + 1, :], (rows, 128))
    rate = outer_rate * (1.0 + outer_momentum)
    for d in range(paths):
        for r in range(CAP):
            m = module_ref[(me ^ d) * (CAP + 1) + r]
            step = rate * scale_ref[m][:, :1]
            for c in chunks(width):
                pieces[d][r, :, c] = (base_ref[m, :, c] - step * acc_ref[m, :, c]).astype(
                    jnp.bfloat16
                )


def store_kernel(
    scale_ref, acc_ref, base_ref, past_ref, updated_hbm, velocity_hbm, updated_ref, velocity_ref, sems
):
    rate = outer_rate * (1.0 + outer_momentum)
    owned, _, width = acc_ref.shape
    part = owned // PARTS

    def copies(i):
        at = pl.ds(i * part, part)
        return [
            pltpu.make_async_copy(ref.at[at], hbm.at[at], sems.at[n, i])
            for n, (ref, hbm) in enumerate(
                ((updated_ref, updated_hbm), (velocity_ref, velocity_hbm))
            )
        ]

    for i in range(PARTS):

        def fill(m, _):
            scale = scale_ref[m][:, :1]
            for c in chunks(width):
                delta = scale * acc_ref[m, :, c]
                updated_ref[m, :, c] = base_ref[m, :, c] - rate * delta
                velocity_ref[m, :, c] = outer_momentum * past_ref[m, :, c] + delta
            return 0

        lax.fori_loop(i * part, (i + 1) * part, fill, 0)
        for copy in copies(i):
            copy.start()
    for i in range(PARTS):
        for copy in copies(i):
            copy.wait()


def unpack_kernel(paths, me_ref, places_ref, *rest):
    pieces, (out_ref, sems) = rest[:paths], rest[paths:]
    me = me_ref[0]
    for wait in (False, True):
        for d in range(paths):
            for r in range(CAP):
                k = places_ref[(me ^ d) * CAP + r]

                @pl.when(k >= 0)
                def _():
                    copy = pltpu.make_async_copy(
                        pieces[d].at[r], out_ref.at[0, k], sems.at[d * CAP + r]
                    )
                    if wait:
                        copy.wait()
                    else:
                        copy.start()


def on_device(path_params, global_params, momentum, module_ids, token_counts):
    paths, held = module_ids.shape
    owned, rows, width = global_params.shape
    shards = lax.axis_size("shard")
    me = lax.axis_index("path").astype(jnp.int32).reshape(1)
    module_ids, counts = in_hbm(module_ids, token_counts)
    slots = paths * CAP
    piece = pltpu.VMEM((CAP, rows, width), jnp.bfloat16)
    module = jax.ShapeDtypeStruct((owned, rows, width), jnp.float32)
    held_module = pltpu.VMEM(module.shape, module.dtype)
    tables = [
        jax.ShapeDtypeStruct((paths * (CAP + 1),), jnp.int32),
        jax.ShapeDtypeStruct((paths * (CAP + 1),), jnp.float32),
        jax.ShapeDtypeStruct((owned,), jnp.float32),
    ]
    room = [
        pltpu.VMEM(module.shape, module.dtype),
        pltpu.VMEM(module.shape, module.dtype),
        pltpu.SemaphoreType.DMA((2, PARTS)),
    ]
    limits = pltpu.CompilerParams(vmem_limit_bytes=24 * 1024 * 1024)
    order = sorted(range(1, paths), key=lambda d: (-(d // 2).bit_count(), d % 2, d))

    def exchange(pieces):
        moved = {
            d: lax.ppermute(pieces[d], "path", [(i, i ^ d) for i in range(paths)]) for d in order
        }
        return [moved[d] for d in range(1, paths)]

    places, *packed = pl.pallas_call(
        functools.partial(pack_kernel, paths, owned, [*order, 0]),
        out_shape=[jax.ShapeDtypeStruct((slots,), jnp.int32)] + [piece] * paths,
        in_specs=[SMEM, SMEM, ANY],
        out_specs=[SMEM] + [VMEM] * paths,
        scratch_shapes=[pltpu.SMEM((paths,), jnp.int32), pltpu.SemaphoreType.DMA((slots,))],
        name="pack",
    )(me, module_ids, *in_hbm(path_params.reshape(held, rows, width)))

    arrived = exchange(packed)
    table, weights, total, acc, base = pl.pallas_call(
        early_kernel,
        out_shape=tables + [held_module] * 2,
        in_specs=[SMEM] * 3 + [VMEM] + [ANY] * 2,
        out_specs=[SMEM] * 3 + [VMEM] * 2,
        scratch_shapes=room,
        compiler_params=limits,
        cost_estimate=pl.CostEstimate(flops=10**6, bytes_accessed=12 * 2**20, transcendentals=0),
        name="early",
    )(me, module_ids, counts, *in_vmem(packed[0]), *in_hbm(global_params, momentum))
    acc, squares = pl.pallas_call(
        functools.partial(combine_kernel, paths),
        out_shape=[held_module, jax.ShapeDtypeStruct((owned, 128), jnp.float32)],
        in_specs=[SMEM] * 4 + [VMEM] * paths,
        out_specs=[VMEM] * 2,
        input_output_aliases={4: 0},
        compiler_params=limits,
        name="combine",
    )(me, table, weights, total, *in_vmem(acc, *arrived))
    parts = [squares] + [
        lax.ppermute(squares, "shard", [(i, (i + d) % shards) for i in range(shards)])
        for d in sorted(range(1, shards), key=lambda d: (d != 2, d))
    ]
    scale, *outgoing = pl.pallas_call(
        functools.partial(send_kernel, paths, shards),
        out_shape=[jax.ShapeDtypeStruct((owned, rows, 128), jnp.float32)] + [piece] * paths,
        in_specs=[SMEM] * 3 + [VMEM] * (2 + shards),
        out_specs=[VMEM] * (1 + paths),
        compiler_params=limits,
        name="send",
    )(me, table, total, *in_vmem(acc, base), *parts)
    returned = [outgoing[0], *exchange(outgoing)]
    updated, velocity = pl.pallas_call(
        store_kernel,
        out_shape=[module] * 2,
        in_specs=[VMEM] * 4,
        out_specs=[ANY] * 2,
        scratch_shapes=room,
        compiler_params=limits,
        cost_estimate=pl.CostEstimate(flops=10**6, bytes_accessed=12 * 2**20, transcendentals=0),
        name="store",
    )(scale, *in_vmem(acc, base), momentum)
    path_out = pl.pallas_call(
        functools.partial(unpack_kernel, paths),
        out_shape=jax.ShapeDtypeStruct(path_params.shape, path_params.dtype),
        in_specs=[SMEM] * 2 + [VMEM] * paths,
        out_specs=ANY,
        scratch_shapes=[pltpu.SemaphoreType.DMA((slots,))],
        name="unpack",
    )(me, places, *in_vmem(*returned))
    return updated, velocity, path_out


def solution(mesh):
    placed = (
        P("path", None, "shard", None),
        P("path", "shard", None),
        P("path", "shard", None),
        P(),
        P(),
    )
    return jax.shard_map(
        on_device,
        mesh=mesh,
        in_specs=placed,
        out_specs=(
            P("path", "shard", None),
            P("path", "shard", None),
            P("path", None, "shard", None),
        ),
        check_vma=False,
    )
```

```python
import functools

import jax
import jax.numpy as jnp
from jax import lax
from jax.experimental import pallas as pl
from jax.experimental.pallas import tpu as pltpu
from jax.sharding import PartitionSpec as P

CAP = 2
CHUNK = 1024
PARTS = 4
outer_momentum = 0.9
outer_rate = 0.7

SMEM = pl.BlockSpec(memory_space=pltpu.SMEM)
VMEM = pl.BlockSpec(memory_space=pltpu.VMEM)
ANY = pl.BlockSpec(memory_space=pl.ANY)


def in_vmem(*arrays):
    return [pltpu.with_memory_space_constraint(x, pltpu.VMEM) for x in arrays]


def in_hbm(*arrays):
    return [pltpu.with_memory_space_constraint(x, pltpu.HBM) for x in arrays]


def chunks(width):
    step = CHUNK if width % CHUNK == 0 else width
    return [pl.ds(at, step) for at in range(0, width, step)]


def fetches(me, sent, local_ref, places_ref, sems):
    found = []
    for n, (d, parity, piece) in enumerate(sent):
        wanted = True if parity is None else lax.rem(me ^ d, 2) == parity
        for r in range(CAP):
            k = jnp.maximum(places_ref[(me ^ d) * CAP + r], 0)
            copy = pltpu.make_async_copy(local_ref.at[k], piece.at[r], sems.at[n * CAP + r])
            found.append((wanted, copy))
    return found


def run(wanted, act):
    if wanted is True:
        act()
    else:
        pl.when(wanted)(act)


def pack_kernel(
    owned, sent, me_ref, ids_ref, counts_ref, local_ref,
    places_ref, module_ref, weight_ref, total_ref, *rest,
):
    pieces, (seen, sems) = rest[:-2], rest[-2:]
    me = me_ref[0]
    paths, held = ids_ref.shape
    for i in range(paths):
        seen[i] = jnp.int32(0)
    for i in range(paths * CAP):
        places_ref[i] = jnp.int32(-1)
    for k in range(held):
        group = lax.div(ids_ref[me, k], jnp.int32(owned))
        rank = seen[group]
        seen[group] = rank + 1
        places_ref[group * CAP + rank] = jnp.int32(k)
    sent = [(*s, p) for s, p in zip(sent, pieces, strict=True)]
    copies = fetches(me, sent, local_ref, places_ref, sems)
    for wanted, copy in copies:
        run(wanted, copy.start)
    find_slots(me, owned, ids_ref, counts_ref, module_ref, weight_ref, total_ref)
    for wanted, copy in copies:
        run(wanted, copy.wait)


def find_slots(me, owned, ids_ref, counts_ref, module_ref, weight_ref, total_ref):
    paths, held = ids_ref.shape

    def reset(i, _):
        total_ref[i] = jnp.float32(0.0)
        return 0

    def one(path, _):
        first = path * (CAP + 1)
        for r in range(CAP):
            module_ref[first + r] = jnp.int32(0)
            weight_ref[first + r] = jnp.float32(0.0)
        rank = jnp.int32(0)
        for k in range(held):
            at = ids_ref[path, k] - me * owned
            mine = (at >= 0) & (at < owned)
            slot = first + jnp.where(mine, rank, CAP)
            module_ref[slot] = at
            weight_ref[slot] = counts_ref[path, k].astype(jnp.float32)
            rank = rank + mine.astype(jnp.int32)
        for r in range(CAP):
            at = module_ref[first + r]
            total_ref[at] = total_ref[at] + weight_ref[first + r]
        return 0

    lax.fori_loop(0, owned, reset, 0)
    lax.fori_loop(0, paths, one, 0)


def subtract(me, pieces, distances, module_ref, weight_ref, acc_ref):
    width = acc_ref.shape[2]
    for piece, d in zip(pieces, distances, strict=True):
        for r in range(CAP):
            slot = (me ^ d) * (CAP + 1) + r
            m, weight = module_ref[slot], weight_ref[slot]
            for c in chunks(width):
                acc_ref[m, :, c] = acc_ref[m, :, c] - weight * piece[r, :, c].astype(jnp.float32)


def combine(parity, me, distances, pieces, tables, params_hbm, acc_ref, squares_ref, params_ref, sems):
    module_ref, weight_ref, total_ref = tables
    owned, rows, width = acc_ref.shape
    part = owned // PARTS

    def copy(i):
        at = pl.ds(i * part, part)
        return pltpu.make_async_copy(params_hbm.at[at], params_ref.at[at], sems.at[i])

    @pl.when(lax.rem(me, 2) == parity)
    def _():
        for i in range(PARTS):
            copy(i).start()

        def clear(m, _):
            acc_ref[m] = jnp.zeros((rows, width), jnp.float32)
            return 0

        lax.fori_loop(0, owned, clear, 0)
        subtract(me, pieces, distances, module_ref, weight_ref, acc_ref)
        for m in range(owned):
            if m % part == 0:
                copy(m // part).wait()
            total = jnp.full((rows, 128), total_ref[m], jnp.float32)
            inverse = 1.0 / jnp.maximum(total, 1.0)
            added = jnp.zeros((rows, 128), jnp.float32)
            for at in range(0, width, 128):
                c = pl.ds(at, 128)
                acc = acc_ref[m, :, c] + total * params_ref[m, :, c]
                acc_ref[m, :, c] = acc
                raw = acc * inverse
                added = added + raw * raw
            squares_ref[pl.ds(m, 1), :] = jnp.sum(added, axis=0, keepdims=True)


def first_combine_kernel(
    distances, sent, me_ref, module_ref, weight_ref, total_ref, places_ref, local_ref, params_hbm, *rest
):
    n = len(distances)
    arrived, (acc_ref, squares_ref, *pieces), room = rest[:n], rest[n:-3], rest[-3:]
    params_room, params_sems, sems = room
    me = me_ref[0]
    sent = [(*s, p) for s, p in zip(sent, pieces, strict=True)]
    copies = fetches(me, sent, local_ref, places_ref, sems)
    for wanted, copy in copies:
        run(wanted, copy.start)
    for wanted, copy in copies:
        run(wanted, copy.wait)
    tables = module_ref, weight_ref, total_ref
    combine(
        0, me, distances, arrived, tables, params_hbm, acc_ref, squares_ref, params_room, params_sems
    )


def second_combine_kernel(
    distances, me_ref, module_ref, weight_ref, total_ref, acc_in, params_hbm, *rest
):
    arrived, (acc_ref, squares_ref, *room) = rest[:-4], rest[-4:]
    tables = module_ref, weight_ref, total_ref
    combine(1, me_ref[0], distances, arrived, tables, params_hbm, acc_ref, squares_ref, *room)


def scales(entries, total, squares):
    inverse = 1.0 / jnp.maximum(total, 1.0)
    mean = jnp.sum(squares, axis=1, keepdims=True) / entries
    factor = jnp.minimum(1.0, 1.0 / jnp.sqrt(mean + 1e-06))
    return inverse * factor


def step(scale, acc, params, past):
    delta = scale * acc
    velocity = outer_momentum * past + delta
    return params - outer_rate * (outer_momentum * velocity + delta), velocity


def send_kernel(
    order, shards, me_ref, module_ref, total_ref, acc_ref, params_ref, past_ref, *rest
):
    even, odd, (scale_ref, *pieces) = rest[:shards], rest[shards : 2 * shards], rest[2 * shards :]
    me = me_ref[0]
    owned, rows, width = acc_ref.shape
    is_odd = lax.rem(me, 2) == 1
    summed = jnp.where(is_odd, odd[0][...], even[0][...])
    for a, b in zip(even[1:], odd[1:], strict=True):
        summed = summed + jnp.where(is_odd, b[...], a[...])
    total = jnp.concatenate(
        [jnp.full((1, 128), total_ref[m], jnp.float32) for m in range(owned)], axis=0
    )
    scale = scales(rows * width * shards, total, summed)
    for m in range(owned):
        scale_ref[m] = jnp.broadcast_to(scale[m : m + 1, :], (rows, 128))
    for d, piece in zip(order, pieces, strict=True):
        for r in range(CAP):
            m = module_ref[(me ^ d) * (CAP + 1) + r]
            scale_m = scale_ref[m][:, :1]
            for c in chunks(width):
                updated, _ = step(
                    scale_m, acc_ref[m, :, c], params_ref[m, :, c], past_ref[m, :, c]
                )
                piece[r, :, c] = updated.astype(jnp.bfloat16)


def store_kernel(
    scale_ref, acc_ref, params_ref, past_ref, updated_hbm, velocity_hbm, updated_ref, velocity_ref, sems
):
    owned, _, width = acc_ref.shape
    part = owned // PARTS

    def copies(i):
        at = pl.ds(i * part, part)
        return [
            pltpu.make_async_copy(ref.at[at], hbm.at[at], sems.at[n, i])
            for n, (ref, hbm) in enumerate(
                ((updated_ref, updated_hbm), (velocity_ref, velocity_hbm))
            )
        ]

    for i in range(PARTS):

        def fill(m, _):
            scale = scale_ref[m][:, :1]
            for c in chunks(width):
                updated_ref[m, :, c], velocity_ref[m, :, c] = step(
                    scale, acc_ref[m, :, c], params_ref[m, :, c], past_ref[m, :, c]
                )
            return 0

        lax.fori_loop(i * part, (i + 1) * part, fill, 0)
        for copy in copies(i):
            copy.start()
    for i in range(PARTS):
        for copy in copies(i):
            copy.wait()


def unpack_kernel(order, me_ref, places_ref, *rest):
    pieces, (out_ref, sems) = rest[:-2], rest[-2:]
    me = me_ref[0]
    for wait in (False, True):
        for d, piece in zip(order, pieces, strict=True):
            for r in range(CAP):
                k = places_ref[(me ^ d) * CAP + r]

                @pl.when(k >= 0)
                def _():
                    copy = pltpu.make_async_copy(
                        piece.at[r], out_ref.at[0, k], sems.at[d * CAP + r]
                    )
                    if wait:
                        copy.wait()
                    else:
                        copy.start()


def on_device(path_params, global_params, momentum, module_ids, token_counts):
    paths, held = module_ids.shape
    owned, rows, width = global_params.shape
    shards = lax.axis_size("shard")
    me = lax.axis_index("path").astype(jnp.int32).reshape(1)
    module_ids, counts = in_hbm(module_ids, token_counts)
    slots = paths * CAP
    piece = pltpu.VMEM((CAP, rows, width), jnp.bfloat16)
    module = jax.ShapeDtypeStruct((owned, rows, width), jnp.float32)
    held_module = pltpu.VMEM(module.shape, module.dtype)
    tables = [
        jax.ShapeDtypeStruct((paths * (CAP + 1),), jnp.int32),
        jax.ShapeDtypeStruct((paths * (CAP + 1),), jnp.float32),
        jax.ShapeDtypeStruct((owned,), jnp.float32),
    ]
    room = [
        pltpu.VMEM(module.shape, module.dtype),
        pltpu.VMEM(module.shape, module.dtype),
        pltpu.SemaphoreType.DMA((2, PARTS)),
    ]
    limits = pltpu.CompilerParams(vmem_limit_bytes=24 * 1024 * 1024)
    far = sorted(range(2, paths, 2), key=lambda d: (-d.bit_count(), d))
    order = far + [d + 1 for d in far] + [1]
    local, params = in_hbm(path_params.reshape(held, rows, width), global_params)

    first = [(d, 0) for d in far] + [(d, None) for d in order[len(far) :]] + [(0, None)]
    third = [(d, 1) for d in far]

    def to_parity(x, d, parity):
        return lax.ppermute(
            x, "path", [(i, i ^ d) for i in range(paths) if (i ^ d) % 2 == parity]
        )

    def sems(sent):
        return pltpu.SemaphoreType.DMA((len(sent) * CAP,))

    places, table, weights, total, *packed = pl.pallas_call(
        functools.partial(pack_kernel, owned, first),
        out_shape=[jax.ShapeDtypeStruct((slots,), jnp.int32)] + tables + [piece] * len(first),
        in_specs=[SMEM] * 3 + [ANY],
        out_specs=[SMEM] * 4 + [VMEM] * len(first),
        scratch_shapes=[pltpu.SMEM((paths,), jnp.int32), sems(first)],
        name="pack",
    )(me, module_ids, counts, local)
    own = packed[-1]
    arrived = [to_parity(x, d, 0) for d, x in zip(order, packed)]
    acc, squares, *repacked = pl.pallas_call(
        functools.partial(first_combine_kernel, [*order, 0], third),
        out_shape=[held_module, jax.ShapeDtypeStruct((owned, 128), jnp.float32)]
        + [piece] * len(third),
        in_specs=[SMEM] * 5 + [ANY] * 2 + [VMEM] * (1 + len(order)),
        out_specs=[VMEM] * (2 + len(third)),
        scratch_shapes=[
            pltpu.VMEM(module.shape, module.dtype),
            pltpu.SemaphoreType.DMA((PARTS,)),
            sems(third),
        ],
        compiler_params=limits,
        name="combine",
    )(me, table, weights, total, places, local, params, *in_vmem(*arrived, own))
    late = order[len(far) :] + far
    arrived = [to_parity(x, d, 1) for d, x in zip(late, packed[len(far) : -1] + repacked)]

    def gather(x, parity):
        turns = sorted(range(1, shards), key=lambda d: (d != 2, d))
        return [x] + [
            lax.ppermute(
                x,
                ("path", "shard"),
                [
                    (p * shards + i, p * shards + (i + d) % shards)
                    for p in range(parity, paths, 2)
                    for i in range(shards)
                ],
            )
            for d in turns
        ]

    parts = gather(squares, 0)
    acc, squares = pl.pallas_call(
        functools.partial(second_combine_kernel, [*late, 0]),
        out_shape=[held_module, jax.ShapeDtypeStruct((owned, 128), jnp.float32)],
        in_specs=[SMEM] * 4 + [VMEM] + [ANY] + [VMEM] * (1 + len(late)),
        out_specs=[VMEM] * 2,
        input_output_aliases={4: 0},
        scratch_shapes=[
            pltpu.VMEM(module.shape, module.dtype),
            pltpu.SemaphoreType.DMA((PARTS,)),
        ],
        compiler_params=limits,
        name="combine",
    )(me, table, weights, total, *in_vmem(acc), params, *in_vmem(*arrived, own))
    parts += gather(squares, 1)
    scale, *outgoing = pl.pallas_call(
        functools.partial(send_kernel, [*order, 0], shards),
        out_shape=[jax.ShapeDtypeStruct((owned, rows, 128), jnp.float32)] + [piece] * paths,
        in_specs=[SMEM] * 3 + [VMEM] * (3 + 2 * shards),
        out_specs=[VMEM] * (1 + paths),
        compiler_params=limits,
        name="send",
    )(me, table, total, *in_vmem(acc), global_params, momentum, *parts)
    returned = [
        lax.ppermute(x, "path", [(i, i ^ d) for i in range(paths)])
        for d, x in zip(order, outgoing)
    ] + [outgoing[-1]]
    updated, velocity = pl.pallas_call(
        store_kernel,
        out_shape=[module] * 2,
        in_specs=[VMEM] * 4,
        out_specs=[ANY] * 2,
        scratch_shapes=room,
        compiler_params=limits,
        cost_estimate=pl.CostEstimate(flops=10**6, bytes_accessed=12 * 2**20, transcendentals=0),
        name="store",
    )(scale, *in_vmem(acc), global_params, momentum)
    path_out = pl.pallas_call(
        functools.partial(unpack_kernel, [*order, 0]),
        out_shape=jax.ShapeDtypeStruct(path_params.shape, path_params.dtype),
        in_specs=[SMEM] * 2 + [VMEM] * paths,
        out_specs=ANY,
        scratch_shapes=[pltpu.SemaphoreType.DMA((slots,))],
        name="unpack",
    )(me, places, *in_vmem(*returned))
    return updated, velocity, path_out


def solution(mesh):
    placed = (
        P("path", None, "shard", None),
        P("path", "shard", None),
        P("path", "shard", None),
        P(),
        P(),
    )
    return jax.shard_map(
        on_device,
        mesh=mesh,
        in_specs=placed,
        out_specs=(
            P("path", "shard", None),
            P("path", "shard", None),
            P("path", None, "shard", None),
        ),
        check_vma=False,
    )
```

```python
import functools

import jax
import jax.numpy as jnp
from jax import lax
from jax.experimental import pallas as pl
from jax.experimental.pallas import tpu as pltpu
from jax.sharding import PartitionSpec as P

CAP = 2
CHUNK = 1024
PARTS = 4
outer_momentum = 0.9
outer_rate = 0.7

SMEM = pl.BlockSpec(memory_space=pltpu.SMEM)
VMEM = pl.BlockSpec(memory_space=pltpu.VMEM)
ANY = pl.BlockSpec(memory_space=pl.ANY)


def in_vmem(*arrays):
    return [pltpu.with_memory_space_constraint(x, pltpu.VMEM) for x in arrays]


def in_hbm(*arrays):
    return [pltpu.with_memory_space_constraint(x, pltpu.HBM) for x in arrays]


def chunks(width):
    step = CHUNK if width % CHUNK == 0 else width
    return [pl.ds(at, step) for at in range(0, width, step)]


def pack_kernel(owned, order, me_ref, ids_ref, local_ref, places_ref, *rest):
    pieces, (seen, sems) = rest[:-2], rest[-2:]
    me = me_ref[0]
    paths = len(order)
    for i in range(paths):
        seen[i] = jnp.int32(0)
    for i in range(paths * CAP):
        places_ref[i] = jnp.int32(-1)
    for k in range(ids_ref.shape[1]):
        group = lax.div(ids_ref[me, k], jnp.int32(owned))
        rank = seen[group]
        seen[group] = rank + 1
        places_ref[group * CAP + rank] = jnp.int32(k)
    copies = []
    for d, piece in zip(order, pieces, strict=True):
        for r in range(CAP):
            k = jnp.maximum(places_ref[(me ^ d) * CAP + r], 0)
            copy = pltpu.make_async_copy(
                local_ref.at[k], piece.at[r], sems.at[d * CAP + r]
            )
            copy.start()
            copies.append(copy)
    for copy in copies:
        copy.wait()


def find_slots(me, owned, ids_ref, counts_ref, module_ref, weight_ref, total_ref):
    paths, held = ids_ref.shape

    def reset(i, _):
        total_ref[i] = jnp.float32(0.0)
        return 0

    def one(path, _):
        first = path * (CAP + 1)
        for r in range(CAP):
            module_ref[first + r] = jnp.int32(0)
            weight_ref[first + r] = jnp.float32(0.0)
        rank = jnp.int32(0)
        for k in range(held):
            at = ids_ref[path, k] - me * owned
            mine = (at >= 0) & (at < owned)
            slot = first + jnp.where(mine, rank, CAP)
            module_ref[slot] = at
            weight_ref[slot] = counts_ref[path, k].astype(jnp.float32)
            rank = rank + mine.astype(jnp.int32)
        for r in range(CAP):
            at = module_ref[first + r]
            total_ref[at] = total_ref[at] + weight_ref[first + r]
        return 0

    lax.fori_loop(0, owned, reset, 0)
    lax.fori_loop(0, paths, one, 0)


def subtract(me, pieces, distances, module_ref, weight_ref, acc_ref):
    width = acc_ref.shape[2]
    for piece, d in zip(pieces, distances, strict=True):
        for r in range(CAP):
            slot = (me ^ d) * (CAP + 1) + r
            m, weight = module_ref[slot], weight_ref[slot]
            for c in chunks(width):
                acc_ref[m, :, c] = acc_ref[m, :, c] - weight * piece[r, :, c].astype(jnp.float32)


def prepare(me, own_ref, params_hbm, past_hbm, tables, acc_ref, base_ref, params_ref, past_ref, sems, find):
    owned, _, width = acc_ref.shape
    part = owned // PARTS

    def copies(i):
        at = pl.ds(i * part, part)
        return [
            pltpu.make_async_copy(hbm.at[at], ref.at[at], sems.at[n, i])
            for n, (hbm, ref) in enumerate(((params_hbm, params_ref), (past_hbm, past_ref)))
        ]

    for i in range(PARTS):
        for copy in copies(i):
            copy.start()
    find()
    module_ref, weight_ref, total_ref = tables
    for i in range(PARTS):
        for copy in copies(i):
            copy.wait()

        def fill(m, _):
            for c in chunks(width):
                params = params_ref[m, :, c]
                acc_ref[m, :, c] = total_ref[m] * params
                base_ref[m, :, c] = params - (outer_rate * outer_momentum**2) * past_ref[m, :, c]
            return 0

        lax.fori_loop(i * part, (i + 1) * part, fill, 0)
    subtract(me, [own_ref], [0], module_ref, weight_ref, acc_ref)


def early_kernel(
    me_ref, ids_ref, counts_ref, own_ref, params_hbm, past_hbm,
    module_ref, weight_ref, total_ref, acc_ref, base_ref, params_ref, past_ref, sems,
):
    me = me_ref[0]
    tables = module_ref, weight_ref, total_ref
    find = functools.partial(find_slots, me, acc_ref.shape[0], ids_ref, counts_ref, *tables)
    prepare(
        me, own_ref, params_hbm, past_hbm, tables, acc_ref, base_ref, params_ref, past_ref, sems, find
    )


def combine_kernel(order, me_ref, module_ref, weight_ref, total_ref, acc_in, *rest):
    pieces, (acc_ref, squares_ref) = rest[:-2], rest[-2:]
    subtract(me_ref[0], pieces, order, module_ref, weight_ref, acc_ref)
    owned, rows, width = acc_ref.shape
    for m in range(owned):
        inverse = 1.0 / jnp.maximum(jnp.full((rows, 128), total_ref[m], jnp.float32), 1.0)
        added = jnp.zeros((rows, 128), jnp.float32)
        for at in range(0, width, 128):
            raw = acc_ref[m, :, pl.ds(at, 128)] * inverse
            added = added + raw * raw
        squares_ref[pl.ds(m, 1), :] = jnp.sum(added, axis=0, keepdims=True)


def scales(entries, total, squares):
    inverse = 1.0 / jnp.maximum(total, 1.0)
    mean = jnp.sum(squares, axis=1, keepdims=True) / entries
    factor = jnp.minimum(1.0, 1.0 / jnp.sqrt(mean + 1e-06))
    return inverse * factor


def send_kernel(order, shards, me_ref, module_ref, total_ref, acc_ref, base_ref, *rest):
    squares, (scale_ref, *pieces) = rest[:shards], rest[shards:]
    me = me_ref[0]
    owned, rows, width = acc_ref.shape
    summed = squares[0][...]
    for other in squares[1:]:
        summed = summed + other[...]
    total = jnp.concatenate(
        [jnp.full((1, 128), total_ref[m], jnp.float32) for m in range(owned)], axis=0
    )
    scale = scales(rows * width * shards, total, summed)
    for m in range(owned):
        scale_ref[m] = jnp.broadcast_to(scale[m : m + 1, :], (rows, 128))
    rate = outer_rate * (1.0 + outer_momentum)
    for d, piece in zip(order, pieces, strict=True):
        for r in range(CAP):
            m = module_ref[(me ^ d) * (CAP + 1) + r]
            step = rate * scale_ref[m][:, :1]
            for c in chunks(width):
                piece[r, :, c] = (base_ref[m, :, c] - step * acc_ref[m, :, c]).astype(
                    jnp.bfloat16
                )


def store_kernel(
    scale_ref, acc_ref, base_ref, past_ref, updated_hbm, velocity_hbm, updated_ref, velocity_ref, sems
):
    rate = outer_rate * (1.0 + outer_momentum)
    owned, _, width = acc_ref.shape
    part = owned // PARTS

    def copies(i):
        at = pl.ds(i * part, part)
        return [
            pltpu.make_async_copy(ref.at[at], hbm.at[at], sems.at[n, i])
            for n, (ref, hbm) in enumerate(
                ((updated_ref, updated_hbm), (velocity_ref, velocity_hbm))
            )
        ]

    for i in range(PARTS):

        def fill(m, _):
            scale = scale_ref[m][:, :1]
            for c in chunks(width):
                delta = scale * acc_ref[m, :, c]
                updated_ref[m, :, c] = base_ref[m, :, c] - rate * delta
                velocity_ref[m, :, c] = outer_momentum * past_ref[m, :, c] + delta
            return 0

        lax.fori_loop(i * part, (i + 1) * part, fill, 0)
        for copy in copies(i):
            copy.start()
    for i in range(PARTS):
        for copy in copies(i):
            copy.wait()


def unpack_kernel(order, me_ref, places_ref, *rest):
    pieces, (out_ref, sems) = rest[:-2], rest[-2:]
    me = me_ref[0]
    for wait in (False, True):
        for d, piece in zip(order, pieces, strict=True):
            for r in range(CAP):
                k = places_ref[(me ^ d) * CAP + r]

                @pl.when(k >= 0)
                def _():
                    copy = pltpu.make_async_copy(
                        piece.at[r], out_ref.at[0, k], sems.at[d * CAP + r]
                    )
                    if wait:
                        copy.wait()
                    else:
                        copy.start()


def on_device(path_params, global_params, momentum, module_ids, token_counts):
    paths, held = module_ids.shape
    owned, rows, width = global_params.shape
    shards = lax.axis_size("shard")
    me = lax.axis_index("path").astype(jnp.int32).reshape(1)
    module_ids, counts = in_hbm(module_ids, token_counts)
    slots = paths * CAP
    piece = pltpu.VMEM((CAP, rows, width), jnp.bfloat16)
    module = jax.ShapeDtypeStruct((owned, rows, width), jnp.float32)
    held_module = pltpu.VMEM(module.shape, module.dtype)
    tables = [
        jax.ShapeDtypeStruct((paths * (CAP + 1),), jnp.int32),
        jax.ShapeDtypeStruct((paths * (CAP + 1),), jnp.float32),
        jax.ShapeDtypeStruct((owned,), jnp.float32),
    ]
    room = [
        pltpu.VMEM(module.shape, module.dtype),
        pltpu.VMEM(module.shape, module.dtype),
        pltpu.SemaphoreType.DMA((2, PARTS)),
    ]
    limits = pltpu.CompilerParams(vmem_limit_bytes=24 * 1024 * 1024)
    far = sorted(range(2, paths, 2), key=lambda d: (-d.bit_count(), -d))
    order = far + [d + 1 for d in far] + [1]

    def exchange(pieces):
        return [
            lax.ppermute(x, "path", [(i, i ^ d) for i in range(paths)])
            for d, x in zip(order, pieces)
        ]

    places, *packed = pl.pallas_call(
        functools.partial(pack_kernel, owned, [*order, 0]),
        out_shape=[jax.ShapeDtypeStruct((slots,), jnp.int32)] + [piece] * paths,
        in_specs=[SMEM, SMEM, ANY],
        out_specs=[SMEM] + [VMEM] * paths,
        scratch_shapes=[pltpu.SMEM((paths,), jnp.int32), pltpu.SemaphoreType.DMA((slots,))],
        name="pack",
    )(me, module_ids, *in_hbm(path_params.reshape(held, rows, width)))

    arrived = exchange(packed)
    table, weights, total, acc, base = pl.pallas_call(
        early_kernel,
        out_shape=tables + [held_module] * 2,
        in_specs=[SMEM] * 3 + [VMEM] + [ANY] * 2,
        out_specs=[SMEM] * 3 + [VMEM] * 2,
        scratch_shapes=room,
        compiler_params=limits,
        cost_estimate=pl.CostEstimate(flops=10**6, bytes_accessed=12 * 2**20, transcendentals=0),
        name="early",
    )(me, module_ids, counts, *in_vmem(packed[-1]), *in_hbm(global_params, momentum))
    acc, squares = pl.pallas_call(
        functools.partial(combine_kernel, order),
        out_shape=[held_module, jax.ShapeDtypeStruct((owned, 128), jnp.float32)],
        in_specs=[SMEM] * 4 + [VMEM] * paths,
        out_specs=[VMEM] * 2,
        input_output_aliases={4: 0},
        compiler_params=limits,
        name="combine",
    )(me, table, weights, total, *in_vmem(acc, *arrived))
    parts = [squares] + [
        lax.ppermute(squares, "shard", [(i, (i + d) % shards) for i in range(shards)])
        for d in sorted(range(1, shards), key=lambda d: (d != 2, d))
    ]
    scale, *outgoing = pl.pallas_call(
        functools.partial(send_kernel, [*order, 0], shards),
        out_shape=[jax.ShapeDtypeStruct((owned, rows, 128), jnp.float32)] + [piece] * paths,
        in_specs=[SMEM] * 3 + [VMEM] * (2 + shards),
        out_specs=[VMEM] * (1 + paths),
        compiler_params=limits,
        name="send",
    )(me, table, total, *in_vmem(acc, base), *parts)
    returned = [*exchange(outgoing), outgoing[-1]]
    updated, velocity = pl.pallas_call(
        store_kernel,
        out_shape=[module] * 2,
        in_specs=[VMEM] * 4,
        out_specs=[ANY] * 2,
        scratch_shapes=room,
        compiler_params=limits,
        cost_estimate=pl.CostEstimate(flops=10**6, bytes_accessed=12 * 2**20, transcendentals=0),
        name="store",
    )(scale, *in_vmem(acc, base), momentum)
    path_out = pl.pallas_call(
        functools.partial(unpack_kernel, [*order, 0]),
        out_shape=jax.ShapeDtypeStruct(path_params.shape, path_params.dtype),
        in_specs=[SMEM] * 2 + [VMEM] * paths,
        out_specs=ANY,
        scratch_shapes=[pltpu.SemaphoreType.DMA((slots,))],
        name="unpack",
    )(me, places, *in_vmem(*returned))
    return updated, velocity, path_out


def solution(mesh):
    placed = (
        P("path", None, "shard", None),
        P("path", "shard", None),
        P("path", "shard", None),
        P(),
        P(),
    )
    return jax.shard_map(
        on_device,
        mesh=mesh,
        in_specs=placed,
        out_specs=(
            P("path", "shard", None),
            P("path", "shard", None),
            P("path", None, "shard", None),
        ),
        check_vma=False,
    )
```

```python
import functools

import jax
import jax.numpy as jnp
from jax import lax
from jax.experimental import pallas as pl
from jax.experimental.pallas import tpu as pltpu
from jax.sharding import PartitionSpec as P

CAP = 2
CHUNK = 1024
PARTS = 4
outer_momentum = 0.9
outer_rate = 0.7

SMEM = pl.BlockSpec(memory_space=pltpu.SMEM)
VMEM = pl.BlockSpec(memory_space=pltpu.VMEM)
ANY = pl.BlockSpec(memory_space=pl.ANY)


def in_vmem(*arrays):
    return [pltpu.with_memory_space_constraint(x, pltpu.VMEM) for x in arrays]


def in_smem(*arrays):
    return [pltpu.with_memory_space_constraint(x, pltpu.SMEM) for x in arrays]


def in_hbm(*arrays):
    return [pltpu.with_memory_space_constraint(x, pltpu.HBM) for x in arrays]


def chunks(width):
    step = CHUNK if width % CHUNK == 0 else width
    return [pl.ds(at, step) for at in range(0, width, step)]


def pack_kernel(owned, order, ids_ref, local_ref, places_ref, *rest):
    pieces, (seen, sems) = rest[:-2], rest[-2:]
    me = lax.axis_index("path").astype(jnp.int32)
    paths = len(order)
    for i in range(paths):
        seen[i] = jnp.int32(0)
    for i in range(paths * CAP):
        places_ref[i] = jnp.int32(-1)
    for k in range(ids_ref.shape[1]):
        group = lax.div(ids_ref[me, k], jnp.int32(owned))
        rank = seen[group]
        seen[group] = rank + 1
        places_ref[group * CAP + rank] = jnp.int32(k)
    copies = []
    for d, piece in zip(order, pieces, strict=True):
        for r in range(CAP):
            k = jnp.maximum(places_ref[(me ^ d) * CAP + r], 0)
            copy = pltpu.make_async_copy(
                local_ref.at[k], piece.at[r], sems.at[d * CAP + r]
            )
            copy.start()
            copies.append(copy)
    for copy in copies:
        copy.wait()


def find_slots(me, owned, ids_ref, counts_ref, module_ref, weight_ref, total_ref):
    paths, held = ids_ref.shape

    def reset(i, _):
        total_ref[i] = jnp.float32(0.0)
        return 0

    def one(path, _):
        first = path * (CAP + 1)
        for r in range(CAP):
            module_ref[first + r] = jnp.int32(0)
            weight_ref[first + r] = jnp.float32(0.0)
        rank = jnp.int32(0)
        for k in range(held):
            at = ids_ref[path, k] - me * owned
            mine = (at >= 0) & (at < owned)
            slot = first + jnp.where(mine, rank, CAP)
            module_ref[slot] = at
            weight_ref[slot] = counts_ref[path, k].astype(jnp.float32)
            rank = rank + mine.astype(jnp.int32)
        for r in range(CAP):
            at = module_ref[first + r]
            total_ref[at] = total_ref[at] + weight_ref[first + r]
        return 0

    lax.fori_loop(0, owned, reset, 0)
    lax.fori_loop(0, paths, one, 0)


def subtract(me, pieces, distances, module_ref, weight_ref, acc_ref):
    width = acc_ref.shape[2]
    for piece, d in zip(pieces, distances, strict=True):
        for r in range(CAP):
            slot = (me ^ d) * (CAP + 1) + r
            m, weight = module_ref[slot], weight_ref[slot]
            for c in chunks(width):
                acc_ref[m, :, c] = acc_ref[m, :, c] - weight * piece[r, :, c].astype(jnp.float32)


def prepare(me, own_ref, params_hbm, past_hbm, tables, acc_ref, base_ref, params_ref, past_ref, sems, find):
    owned, _, width = acc_ref.shape
    part = owned // PARTS

    def copies(i):
        at = pl.ds(i * part, part)
        return [
            pltpu.make_async_copy(hbm.at[at], ref.at[at], sems.at[n, i])
            for n, (hbm, ref) in enumerate(((params_hbm, params_ref), (past_hbm, past_ref)))
        ]

    for i in range(PARTS):
        for copy in copies(i):
            copy.start()
    find()
    module_ref, weight_ref, total_ref = tables
    for i in range(PARTS):
        for copy in copies(i):
            copy.wait()

        def fill(m, _):
            for c in chunks(width):
                params = params_ref[m, :, c]
                acc_ref[m, :, c] = total_ref[m] * params
                base_ref[m, :, c] = params - (outer_rate * outer_momentum**2) * past_ref[m, :, c]
            return 0

        lax.fori_loop(i * part, (i + 1) * part, fill, 0)
    subtract(me, [own_ref], [0], module_ref, weight_ref, acc_ref)


def early_kernel(
    ids_ref, counts_ref, own_ref, params_hbm, past_hbm,
    module_ref, weight_ref, total_ref, acc_ref, base_ref, params_ref, past_ref, sems,
):
    me = lax.axis_index("path").astype(jnp.int32)
    tables = module_ref, weight_ref, total_ref
    find = functools.partial(find_slots, me, acc_ref.shape[0], ids_ref, counts_ref, *tables)
    prepare(
        me, own_ref, params_hbm, past_hbm, tables, acc_ref, base_ref, params_ref, past_ref, sems, find
    )


def combine_kernel(order, module_ref, weight_ref, total_ref, acc_in, *rest):
    pieces, (acc_ref, squares_ref) = rest[:-2], rest[-2:]
    me = lax.axis_index("path").astype(jnp.int32)
    subtract(me, pieces, order, module_ref, weight_ref, acc_ref)
    owned, rows, width = acc_ref.shape
    for m in range(owned):
        inverse = 1.0 / jnp.maximum(jnp.full((rows, 128), total_ref[m], jnp.float32), 1.0)
        added = jnp.zeros((rows, 128), jnp.float32)
        for at in range(0, width, 128):
            raw = acc_ref[m, :, pl.ds(at, 128)] * inverse
            added = added + raw * raw
        squares_ref[pl.ds(m, 1), :] = jnp.sum(added, axis=0, keepdims=True)


def scales(entries, total, squares):
    inverse = 1.0 / jnp.maximum(total, 1.0)
    mean = jnp.sum(squares, axis=1, keepdims=True) / entries
    factor = jnp.minimum(1.0, 1.0 / jnp.sqrt(mean + 1e-06))
    return inverse * factor


def send_kernel(order, shards, module_ref, total_ref, acc_ref, base_ref, *rest):
    squares, (scale_ref, *pieces) = rest[:shards], rest[shards:]
    me = lax.axis_index("path").astype(jnp.int32)
    owned, rows, width = acc_ref.shape
    summed = squares[0][...]
    for other in squares[1:]:
        summed = summed + other[...]
    total = jnp.concatenate(
        [jnp.full((1, 128), total_ref[m], jnp.float32) for m in range(owned)], axis=0
    )
    scale = scales(rows * width * shards, total, summed)
    for m in range(owned):
        scale_ref[m] = jnp.broadcast_to(scale[m : m + 1, :], (rows, 128))
    rate = outer_rate * (1.0 + outer_momentum)
    for d, piece in zip(order, pieces, strict=True):
        for r in range(CAP):
            m = module_ref[(me ^ d) * (CAP + 1) + r]
            step = rate * scale_ref[m][:, :1]
            for c in chunks(width):
                piece[r, :, c] = (base_ref[m, :, c] - step * acc_ref[m, :, c]).astype(
                    jnp.bfloat16
                )


def store_kernel(
    scale_ref, acc_ref, base_ref, past_ref, updated_hbm, velocity_hbm, updated_ref, velocity_ref, sems
):
    rate = outer_rate * (1.0 + outer_momentum)
    owned, _, width = acc_ref.shape
    part = owned // PARTS

    def copies(i):
        at = pl.ds(i * part, part)
        return [
            pltpu.make_async_copy(ref.at[at], hbm.at[at], sems.at[n, i])
            for n, (ref, hbm) in enumerate(
                ((updated_ref, updated_hbm), (velocity_ref, velocity_hbm))
            )
        ]

    for i in range(PARTS):

        def fill(m, _):
            scale = scale_ref[m][:, :1]
            for c in chunks(width):
                delta = scale * acc_ref[m, :, c]
                updated_ref[m, :, c] = base_ref[m, :, c] - rate * delta
                velocity_ref[m, :, c] = outer_momentum * past_ref[m, :, c] + delta
            return 0

        lax.fori_loop(i * part, (i + 1) * part, fill, 0)
        for copy in copies(i):
            copy.start()
    for i in range(PARTS):
        for copy in copies(i):
            copy.wait()


def unpack_kernel(order, places_ref, *rest):
    pieces, (out_ref, sems) = rest[:-2], rest[-2:]
    me = lax.axis_index("path").astype(jnp.int32)
    for wait in (False, True):
        for d, piece in zip(order, pieces, strict=True):
            for r in range(CAP):
                k = places_ref[(me ^ d) * CAP + r]

                @pl.when(k >= 0)
                def _():
                    copy = pltpu.make_async_copy(
                        piece.at[r], out_ref.at[0, k], sems.at[d * CAP + r]
                    )
                    if wait:
                        copy.wait()
                    else:
                        copy.start()


def on_device(path_params, global_params, momentum, module_ids, token_counts):
    paths, held = module_ids.shape
    owned, rows, width = global_params.shape
    shards = lax.axis_size("shard")
    module_ids, counts = in_hbm(module_ids, token_counts)
    slots = paths * CAP
    piece = pltpu.VMEM((CAP, rows, width), jnp.bfloat16)
    module = jax.ShapeDtypeStruct((owned, rows, width), jnp.float32)
    held_module = pltpu.VMEM(module.shape, module.dtype)
    tables = [
        pltpu.SMEM((paths * (CAP + 1),), jnp.int32),
        pltpu.SMEM((paths * (CAP + 1),), jnp.float32),
        pltpu.SMEM((owned,), jnp.float32),
    ]
    room = [
        pltpu.VMEM(module.shape, module.dtype),
        pltpu.VMEM(module.shape, module.dtype),
        pltpu.SemaphoreType.DMA((2, PARTS)),
    ]
    limits = pltpu.CompilerParams(vmem_limit_bytes=24 * 1024 * 1024)
    far = sorted(range(2, paths, 2), key=lambda d: (-d.bit_count(), -d))
    order = far + [d + 1 for d in far[::-1]] + [1]

    def exchange(pieces):
        return [
            lax.ppermute(x, "path", [(i, i ^ d) for i in range(paths)])
            for d, x in zip(order, pieces)
        ]

    places, *packed = pl.pallas_call(
        functools.partial(pack_kernel, owned, [*order, 0]),
        out_shape=[pltpu.SMEM((slots,), jnp.int32)] + [piece] * paths,
        in_specs=[SMEM, ANY],
        out_specs=[SMEM] + [VMEM] * paths,
        scratch_shapes=[pltpu.SMEM((paths,), jnp.int32), pltpu.SemaphoreType.DMA((slots,))],
        name="pack",
    )(module_ids, *in_hbm(path_params.reshape(held, rows, width)))

    arrived = exchange(packed)
    table, weights, total, acc, base = pl.pallas_call(
        early_kernel,
        out_shape=tables + [held_module] * 2,
        in_specs=[SMEM] * 2 + [VMEM] + [ANY] * 2,
        out_specs=[SMEM] * 3 + [VMEM] * 2,
        scratch_shapes=room,
        compiler_params=limits,
        cost_estimate=pl.CostEstimate(flops=10**6, bytes_accessed=12 * 2**20, transcendentals=0),
        name="early",
    )(module_ids, counts, *in_vmem(packed[-1]), *in_hbm(global_params, momentum))
    acc, squares = pl.pallas_call(
        functools.partial(combine_kernel, order),
        out_shape=[held_module, jax.ShapeDtypeStruct((owned, 128), jnp.float32)],
        in_specs=[SMEM] * 3 + [VMEM] * paths,
        out_specs=[VMEM] * 2,
        input_output_aliases={3: 0},
        compiler_params=limits,
        name="combine",
    )(*in_smem(table, weights, total), *in_vmem(acc, *arrived))
    parts = [squares] + [
        lax.ppermute(squares, "shard", [(i, (i + d) % shards) for i in range(shards)])
        for d in sorted(range(1, shards), key=lambda d: (d != 2, d))
    ]
    scale, *outgoing = pl.pallas_call(
        functools.partial(send_kernel, [*order, 0], shards),
        out_shape=[jax.ShapeDtypeStruct((owned, rows, 128), jnp.float32)] + [piece] * paths,
        in_specs=[SMEM] * 2 + [VMEM] * (2 + shards),
        out_specs=[VMEM] * (1 + paths),
        compiler_params=limits,
        name="send",
    )(*in_smem(table, total), *in_vmem(acc, base), *parts)
    returned = [*exchange(outgoing), outgoing[-1]]
    updated, velocity = pl.pallas_call(
        store_kernel,
        out_shape=[module] * 2,
        in_specs=[VMEM] * 4,
        out_specs=[ANY] * 2,
        scratch_shapes=room,
        compiler_params=limits,
        cost_estimate=pl.CostEstimate(flops=10**6, bytes_accessed=12 * 2**20, transcendentals=0),
        name="store",
    )(scale, *in_vmem(acc, base), momentum)
    path_out = pl.pallas_call(
        functools.partial(unpack_kernel, [*order, 0]),
        out_shape=jax.ShapeDtypeStruct(path_params.shape, path_params.dtype),
        in_specs=[SMEM] + [VMEM] * paths,
        out_specs=ANY,
        scratch_shapes=[pltpu.SemaphoreType.DMA((slots,))],
        name="unpack",
    )(*in_smem(places), *in_vmem(*returned))
    return updated, velocity, path_out


def solution(mesh):
    placed = (
        P("path", None, "shard", None),
        P("path", "shard", None),
        P("path", "shard", None),
        P(),
        P(),
    )
    return jax.shard_map(
        on_device,
        mesh=mesh,
        in_specs=placed,
        out_specs=(
            P("path", "shard", None),
            P("path", "shard", None),
            P("path", None, "shard", None),
        ),
        check_vma=False,
    )
```

```python
import functools

import jax
import jax.numpy as jnp
from jax import lax
from jax.experimental import pallas as pl
from jax.experimental.pallas import tpu as pltpu
from jax.sharding import PartitionSpec as P

CAP = 2
CHUNK = 1024
PARTS = 4
outer_momentum = 0.9
outer_rate = 0.7

SMEM = pl.BlockSpec(memory_space=pltpu.SMEM)
VMEM = pl.BlockSpec(memory_space=pltpu.VMEM)
ANY = pl.BlockSpec(memory_space=pl.ANY)


def in_vmem(*arrays):
    return [pltpu.with_memory_space_constraint(x, pltpu.VMEM) for x in arrays]


def in_smem(*arrays):
    return [pltpu.with_memory_space_constraint(x, pltpu.SMEM) for x in arrays]


def in_hbm(*arrays):
    return [pltpu.with_memory_space_constraint(x, pltpu.HBM) for x in arrays]


def chunks(width):
    step = CHUNK if width % CHUNK == 0 else width
    return [pl.ds(at, step) for at in range(0, width, step)]


def pack_kernel(owned, order, ids_hbm, local_hbm, places_ref, *rest):
    pieces, (ids_ref, local_ref, seen, sems) = rest[:-4], rest[-4:]
    me = lax.axis_index("path").astype(jnp.int32)
    paths, held = ids_ref.shape
    part = held // PARTS
    ids_copy = pltpu.make_async_copy(ids_hbm, ids_ref, sems.at[PARTS])
    ids_copy.start()
    copies = []
    for i in range(PARTS):
        at = pl.ds(i * part, part)
        copies.append(pltpu.make_async_copy(local_hbm.at[at], local_ref.at[at], sems.at[i]))
        copies[-1].start()
    for i in range(paths):
        seen[i] = jnp.int32(0)
    for i in range(paths * CAP):
        places_ref[i] = jnp.int32(-1)
    ids_copy.wait()
    for k in range(held):
        group = lax.div(ids_ref[me, k], jnp.int32(owned))
        rank = seen[group]
        seen[group] = rank + 1
        places_ref[group * CAP + rank] = jnp.int32(k)
    for copy in copies:
        copy.wait()
    for d, piece in zip(order, pieces, strict=True):
        for r in range(CAP):
            piece[r] = local_ref[jnp.maximum(places_ref[(me ^ d) * CAP + r], 0)]


def find_slots(me, owned, ids_ref, counts_ref, module_ref, weight_ref, total_ref):
    paths, held = ids_ref.shape

    def reset(i, _):
        total_ref[i] = jnp.float32(0.0)
        return 0

    def one(path, _):
        first = path * (CAP + 1)
        for r in range(CAP):
            module_ref[first + r] = jnp.int32(0)
            weight_ref[first + r] = jnp.float32(0.0)
        rank = jnp.int32(0)
        for k in range(held):
            at = ids_ref[path, k] - me * owned
            mine = (at >= 0) & (at < owned)
            slot = first + jnp.where(mine, rank, CAP)
            module_ref[slot] = at
            weight_ref[slot] = counts_ref[path, k].astype(jnp.float32)
            rank = rank + mine.astype(jnp.int32)
        for r in range(CAP):
            at = module_ref[first + r]
            total_ref[at] = total_ref[at] + weight_ref[first + r]
        return 0

    lax.fori_loop(0, owned, reset, 0)
    lax.fori_loop(0, paths, one, 0)


def subtract(me, pieces, distances, module_ref, weight_ref, acc_ref):
    width = acc_ref.shape[2]
    for piece, d in zip(pieces, distances, strict=True):
        for r in range(CAP):
            slot = (me ^ d) * (CAP + 1) + r
            m, weight = module_ref[slot], weight_ref[slot]
            for c in chunks(width):
                acc_ref[m, :, c] = acc_ref[m, :, c] - weight * piece[r, :, c].astype(jnp.float32)


def prepare(me, own_ref, params_hbm, past_hbm, tables, acc_ref, base_ref, params_ref, past_ref, sems, find):
    owned, _, width = acc_ref.shape
    part = owned // PARTS

    def copies(i):
        at = pl.ds(i * part, part)
        return [
            pltpu.make_async_copy(hbm.at[at], ref.at[at], sems.at[n, i])
            for n, (hbm, ref) in enumerate(((params_hbm, params_ref), (past_hbm, past_ref)))
        ]

    for i in range(PARTS):
        for copy in copies(i):
            copy.start()
    find()
    module_ref, weight_ref, total_ref = tables
    for i in range(PARTS):
        for copy in copies(i):
            copy.wait()

        def fill(m, _):
            for c in chunks(width):
                params = params_ref[m, :, c]
                acc_ref[m, :, c] = total_ref[m] * params
                base_ref[m, :, c] = params - (outer_rate * outer_momentum**2) * past_ref[m, :, c]
            return 0

        lax.fori_loop(i * part, (i + 1) * part, fill, 0)
    subtract(me, [own_ref], [0], module_ref, weight_ref, acc_ref)


def early_kernel(
    ids_ref, counts_ref, own_ref, params_hbm, past_hbm,
    module_ref, weight_ref, total_ref, acc_ref, base_ref, params_ref, past_ref, sems,
):
    me = lax.axis_index("path").astype(jnp.int32)
    tables = module_ref, weight_ref, total_ref
    find = functools.partial(find_slots, me, acc_ref.shape[0], ids_ref, counts_ref, *tables)
    prepare(
        me, own_ref, params_hbm, past_hbm, tables, acc_ref, base_ref, params_ref, past_ref, sems, find
    )


def combine_kernel(order, module_ref, weight_ref, total_ref, acc_in, *rest):
    pieces, (acc_ref, squares_ref) = rest[:-2], rest[-2:]
    me = lax.axis_index("path").astype(jnp.int32)
    subtract(me, pieces, order, module_ref, weight_ref, acc_ref)
    owned, rows, width = acc_ref.shape
    for m in range(owned):
        inverse = 1.0 / jnp.maximum(jnp.full((rows, 128), total_ref[m], jnp.float32), 1.0)
        added = jnp.zeros((rows, 128), jnp.float32)
        for at in range(0, width, 128):
            raw = acc_ref[m, :, pl.ds(at, 128)] * inverse
            added = added + raw * raw
        squares_ref[pl.ds(m, 1), :] = jnp.sum(added, axis=0, keepdims=True)


def scales(entries, total, squares):
    inverse = 1.0 / jnp.maximum(total, 1.0)
    mean = jnp.sum(squares, axis=1, keepdims=True) / entries
    factor = jnp.minimum(1.0, 1.0 / jnp.sqrt(mean + 1e-06))
    return inverse * factor


def send_kernel(order, shards, module_ref, total_ref, acc_ref, base_ref, *rest):
    squares, (scale_ref, *pieces) = rest[:shards], rest[shards:]
    me = lax.axis_index("path").astype(jnp.int32)
    owned, rows, width = acc_ref.shape
    summed = squares[0][...]
    for other in squares[1:]:
        summed = summed + other[...]
    total = jnp.concatenate(
        [jnp.full((1, 128), total_ref[m], jnp.float32) for m in range(owned)], axis=0
    )
    scale = scales(rows * width * shards, total, summed)
    for m in range(owned):
        scale_ref[m] = jnp.broadcast_to(scale[m : m + 1, :], (rows, 128))
    rate = outer_rate * (1.0 + outer_momentum)
    for d, piece in zip(order, pieces, strict=True):
        for r in range(CAP):
            m = module_ref[(me ^ d) * (CAP + 1) + r]
            step = rate * scale_ref[m][:, :1]
            for c in chunks(width):
                piece[r, :, c] = (base_ref[m, :, c] - step * acc_ref[m, :, c]).astype(
                    jnp.bfloat16
                )


def store_kernel(
    scale_ref, acc_ref, base_ref, past_ref, updated_hbm, velocity_hbm, updated_ref, velocity_ref, sems
):
    rate = outer_rate * (1.0 + outer_momentum)
    owned, _, width = acc_ref.shape
    part = owned // PARTS

    def copies(i):
        at = pl.ds(i * part, part)
        return [
            pltpu.make_async_copy(ref.at[at], hbm.at[at], sems.at[n, i])
            for n, (ref, hbm) in enumerate(
                ((updated_ref, updated_hbm), (velocity_ref, velocity_hbm))
            )
        ]

    for i in range(PARTS):

        def fill(m, _):
            scale = scale_ref[m][:, :1]
            for c in chunks(width):
                delta = scale * acc_ref[m, :, c]
                updated_ref[m, :, c] = base_ref[m, :, c] - rate * delta
                velocity_ref[m, :, c] = outer_momentum * past_ref[m, :, c] + delta
            return 0

        lax.fori_loop(i * part, (i + 1) * part, fill, 0)
        for copy in copies(i):
            copy.start()
    for i in range(PARTS):
        for copy in copies(i):
            copy.wait()


def unpack_kernel(order, places_ref, *rest):
    pieces, (out_ref, sems) = rest[:-2], rest[-2:]
    me = lax.axis_index("path").astype(jnp.int32)
    for wait in (False, True):
        for d, piece in zip(order, pieces, strict=True):
            for r in range(CAP):
                k = places_ref[(me ^ d) * CAP + r]

                @pl.when(k >= 0)
                def _():
                    copy = pltpu.make_async_copy(
                        piece.at[r], out_ref.at[0, k], sems.at[d * CAP + r]
                    )
                    if wait:
                        copy.wait()
                    else:
                        copy.start()


def on_device(path_params, global_params, momentum, module_ids, token_counts):
    paths, held = module_ids.shape
    owned, rows, width = global_params.shape
    shards = lax.axis_size("shard")
    module_ids, counts = in_hbm(module_ids, token_counts)
    slots = paths * CAP
    piece = pltpu.VMEM((CAP, rows, width), jnp.bfloat16)
    module = jax.ShapeDtypeStruct((owned, rows, width), jnp.float32)
    held_module = pltpu.VMEM(module.shape, module.dtype)
    tables = [
        pltpu.SMEM((paths * (CAP + 1),), jnp.int32),
        pltpu.SMEM((paths * (CAP + 1),), jnp.float32),
        pltpu.SMEM((owned,), jnp.float32),
    ]
    room = [
        pltpu.VMEM(module.shape, module.dtype),
        pltpu.VMEM(module.shape, module.dtype),
        pltpu.SemaphoreType.DMA((2, PARTS)),
    ]
    limits = pltpu.CompilerParams(vmem_limit_bytes=24 * 1024 * 1024)
    far = sorted(range(2, paths, 2), key=lambda d: (-d.bit_count(), d))
    order = far + [d + 1 for d in far[::-1]] + [1]

    def exchange(pieces):
        return [
            lax.ppermute(x, "path", [(i, i ^ d) for i in range(paths)])
            for d, x in zip(order, pieces)
        ]

    places, *packed = pl.pallas_call(
        functools.partial(pack_kernel, owned, [*order, 0]),
        out_shape=[pltpu.SMEM((slots,), jnp.int32)] + [piece] * paths,
        in_specs=[ANY] * 2,
        out_specs=[SMEM] + [VMEM] * paths,
        scratch_shapes=[
            pltpu.SMEM(module_ids.shape, jnp.int32),
            pltpu.VMEM((held, rows, width), jnp.bfloat16),
            pltpu.SMEM((paths,), jnp.int32),
            pltpu.SemaphoreType.DMA((PARTS + 1,)),
        ],
        compiler_params=limits,
        name="pack",
    )(module_ids, *in_hbm(path_params.reshape(held, rows, width)))

    arrived = exchange(packed)
    table, weights, total, acc, base = pl.pallas_call(
        early_kernel,
        out_shape=tables + [held_module] * 2,
        in_specs=[SMEM] * 2 + [VMEM] + [ANY] * 2,
        out_specs=[SMEM] * 3 + [VMEM] * 2,
        scratch_shapes=room,
        compiler_params=limits,
        cost_estimate=pl.CostEstimate(flops=10**6, bytes_accessed=12 * 2**20, transcendentals=0),
        name="early",
    )(module_ids, counts, *in_vmem(packed[-1]), *in_hbm(global_params, momentum))
    acc, squares = pl.pallas_call(
        functools.partial(combine_kernel, order),
        out_shape=[held_module, jax.ShapeDtypeStruct((owned, 128), jnp.float32)],
        in_specs=[SMEM] * 3 + [VMEM] * paths,
        out_specs=[VMEM] * 2,
        input_output_aliases={3: 0},
        compiler_params=limits,
        name="combine",
    )(*in_smem(table, weights, total), *in_vmem(acc, *arrived))
    parts = [squares] + [
        lax.ppermute(squares, "shard", [(i, (i + d) % shards) for i in range(shards)])
        for d in sorted(range(1, shards), key=lambda d: (d != 2, d))
    ]
    scale, *outgoing = pl.pallas_call(
        functools.partial(send_kernel, [*order, 0], shards),
        out_shape=[jax.ShapeDtypeStruct((owned, rows, 128), jnp.float32)] + [piece] * paths,
        in_specs=[SMEM] * 2 + [VMEM] * (2 + shards),
        out_specs=[VMEM] * (1 + paths),
        compiler_params=limits,
        name="send",
    )(*in_smem(table, total), *in_vmem(acc, base), *parts)
    returned = [*exchange(outgoing), outgoing[-1]]
    updated, velocity = pl.pallas_call(
        store_kernel,
        out_shape=[module] * 2,
        in_specs=[VMEM] * 4,
        out_specs=[ANY] * 2,
        scratch_shapes=room,
        compiler_params=limits,
        cost_estimate=pl.CostEstimate(flops=10**6, bytes_accessed=12 * 2**20, transcendentals=0),
        name="store",
    )(scale, *in_vmem(acc, base), momentum)
    path_out = pl.pallas_call(
        functools.partial(unpack_kernel, [*order, 0]),
        out_shape=jax.ShapeDtypeStruct(path_params.shape, path_params.dtype),
        in_specs=[SMEM] + [VMEM] * paths,
        out_specs=ANY,
        scratch_shapes=[pltpu.SemaphoreType.DMA((slots,))],
        name="unpack",
    )(*in_smem(places), *in_vmem(*returned))
    return updated, velocity, path_out


def solution(mesh):
    placed = (
        P("path", None, "shard", None),
        P("path", "shard", None),
        P("path", "shard", None),
        P(),
        P(),
    )
    return jax.shard_map(
        on_device,
        mesh=mesh,
        in_specs=placed,
        out_specs=(
            P("path", "shard", None),
            P("path", "shard", None),
            P("path", None, "shard", None),
        ),
        check_vma=False,
    )
```

```python
import functools

import jax
import jax.numpy as jnp
from jax import lax
from jax.experimental import pallas as pl
from jax.experimental.pallas import tpu as pltpu
from jax.sharding import PartitionSpec as P

CAP = 2
CHUNK = 1024
PARTS = 4
outer_momentum = 0.9
outer_rate = 0.7

SMEM = pl.BlockSpec(memory_space=pltpu.SMEM)
VMEM = pl.BlockSpec(memory_space=pltpu.VMEM)
ANY = pl.BlockSpec(memory_space=pl.ANY)


def in_vmem(*arrays):
    return [pltpu.with_memory_space_constraint(x, pltpu.VMEM) for x in arrays]


def in_smem(*arrays):
    return [pltpu.with_memory_space_constraint(x, pltpu.SMEM) for x in arrays]


def in_hbm(*arrays):
    return [pltpu.with_memory_space_constraint(x, pltpu.HBM) for x in arrays]


def chunks(width):
    step = CHUNK if width % CHUNK == 0 else width
    return [pl.ds(at, step) for at in range(0, width, step)]


def pack_kernel(owned, order, ids_hbm, local_hbm, places_ref, *rest):
    pieces, (ids_ref, local_ref, seen, sems) = rest[:-4], rest[-4:]
    me = lax.axis_index("path").astype(jnp.int32)
    paths, held = ids_ref.shape
    part = held // PARTS
    ids_copy = pltpu.make_async_copy(ids_hbm, ids_ref, sems.at[PARTS])
    ids_copy.start()
    copies = []
    for i in range(PARTS):
        at = pl.ds(i * part, part)
        copies.append(pltpu.make_async_copy(local_hbm.at[at], local_ref.at[at], sems.at[i]))
        copies[-1].start()
    for i in range(paths):
        seen[i] = jnp.int32(0)
    for i in range(paths * CAP):
        places_ref[i] = jnp.int32(-1)
    ids_copy.wait()
    for k in range(held):
        group = lax.div(ids_ref[me, k], jnp.int32(owned))
        rank = seen[group]
        seen[group] = rank + 1
        places_ref[group * CAP + rank] = jnp.int32(k)
    for copy in copies:
        copy.wait()
    for d, piece in zip(order, pieces, strict=True):
        for r in range(CAP):
            piece[r] = local_ref[jnp.maximum(places_ref[(me ^ d) * CAP + r], 0)]


def find_slots(me, owned, ids_ref, counts_ref, module_ref, weight_ref, total_ref):
    paths, held = ids_ref.shape

    def reset(i, _):
        total_ref[i] = jnp.float32(0.0)
        return 0

    def one(path, _):
        first = path * (CAP + 1)
        for r in range(CAP):
            module_ref[first + r] = jnp.int32(0)
            weight_ref[first + r] = jnp.float32(0.0)
        rank = jnp.int32(0)
        for k in range(held):
            at = ids_ref[path, k] - me * owned
            mine = (at >= 0) & (at < owned)
            slot = first + jnp.where(mine, rank, CAP)
            module_ref[slot] = at
            weight_ref[slot] = counts_ref[path, k].astype(jnp.float32)
            rank = rank + mine.astype(jnp.int32)
        for r in range(CAP):
            at = module_ref[first + r]
            total_ref[at] = total_ref[at] + weight_ref[first + r]
        return 0

    lax.fori_loop(0, owned, reset, 0)
    lax.fori_loop(0, paths, one, 0)


def subtract(me, pieces, distances, module_ref, weight_ref, acc_ref):
    width = acc_ref.shape[2]
    for piece, d in zip(pieces, distances, strict=True):
        for r in range(CAP):
            slot = (me ^ d) * (CAP + 1) + r
            m, weight = module_ref[slot], weight_ref[slot]
            for c in chunks(width):
                acc_ref[m, :, c] = acc_ref[m, :, c] - weight * piece[r, :, c].astype(jnp.float32)


def prepare(me, own_ref, params_hbm, past_hbm, tables, acc_ref, base_ref, params_ref, past_ref, sems, find):
    owned, _, width = acc_ref.shape
    part = owned // PARTS

    def copies(i):
        at = pl.ds(i * part, part)
        return [
            pltpu.make_async_copy(hbm.at[at], ref.at[at], sems.at[n, i])
            for n, (hbm, ref) in enumerate(((params_hbm, params_ref), (past_hbm, past_ref)))
        ]

    for i in range(PARTS):
        for copy in copies(i):
            copy.start()
    find()
    module_ref, weight_ref, total_ref = tables
    for i in range(PARTS):
        for copy in copies(i):
            copy.wait()

        def fill(m, _):
            for c in chunks(width):
                params = params_ref[m, :, c]
                acc_ref[m, :, c] = total_ref[m] * params
                base_ref[m, :, c] = params - (outer_rate * outer_momentum**2) * past_ref[m, :, c]
            return 0

        lax.fori_loop(i * part, (i + 1) * part, fill, 0)
    subtract(me, [own_ref], [0], module_ref, weight_ref, acc_ref)


def early_kernel(
    ids_ref, counts_ref, own_ref, params_hbm, past_hbm,
    module_ref, weight_ref, total_ref, acc_ref, base_ref, params_ref, past_ref, sems,
):
    me = lax.axis_index("path").astype(jnp.int32)
    tables = module_ref, weight_ref, total_ref
    find = functools.partial(find_slots, me, acc_ref.shape[0], ids_ref, counts_ref, *tables)
    prepare(
        me, own_ref, params_hbm, past_hbm, tables, acc_ref, base_ref, params_ref, past_ref, sems, find
    )


def diagonal(owned):
    row = lax.broadcasted_iota(jnp.int32, (owned, 128), 0)
    return row == lax.broadcasted_iota(jnp.int32, (owned, 128), 1)


def combine_kernel(order, module_ref, weight_ref, total_ref, acc_in, *rest):
    pieces, (acc_ref, squares_ref) = rest[:-2], rest[-2:]
    me = lax.axis_index("path").astype(jnp.int32)
    subtract(me, pieces, order, module_ref, weight_ref, acc_ref)
    owned, rows, width = acc_ref.shape
    sums = []
    for m in range(owned):
        inverse = 1.0 / jnp.maximum(jnp.full((rows, 128), total_ref[m], jnp.float32), 1.0)
        added = jnp.zeros((rows, 128), jnp.float32)
        for at in range(0, width, 128):
            raw = acc_ref[m, :, pl.ds(at, 128)] * inverse
            added = added + raw * raw
        sums.append(jnp.sum(added, axis=0, keepdims=True))
    sums = jnp.sum(jnp.concatenate(sums, axis=0), axis=1, keepdims=True)
    squares_ref[...] = jnp.sum(jnp.where(diagonal(owned), sums, 0.0), axis=0, keepdims=True)


def scales(entries, total, squares):
    inverse = 1.0 / jnp.maximum(total, 1.0)
    mean = jnp.sum(squares, axis=1, keepdims=True) / entries
    factor = jnp.minimum(1.0, 1.0 / jnp.sqrt(mean + 1e-06))
    return inverse * factor


def send_kernel(order, shards, module_ref, total_ref, acc_ref, base_ref, *rest):
    squares, (scale_ref, *pieces) = rest[:shards], rest[shards:]
    me = lax.axis_index("path").astype(jnp.int32)
    owned, rows, width = acc_ref.shape
    summed = squares[0][...]
    for other in squares[1:]:
        summed = summed + other[...]
    total = jnp.concatenate(
        [jnp.full((1, 128), total_ref[m], jnp.float32) for m in range(owned)], axis=0
    )
    summed = jnp.where(diagonal(owned), summed, 0.0)
    scale = scales(rows * width * shards, total, summed)
    for m in range(owned):
        scale_ref[m] = jnp.broadcast_to(scale[m : m + 1, :], (rows, 128))
    rate = outer_rate * (1.0 + outer_momentum)
    for d, piece in zip(order, pieces, strict=True):
        for r in range(CAP):
            m = module_ref[(me ^ d) * (CAP + 1) + r]
            step = rate * scale_ref[m][:, :1]
            for c in chunks(width):
                piece[r, :, c] = (base_ref[m, :, c] - step * acc_ref[m, :, c]).astype(
                    jnp.bfloat16
                )


def store_kernel(
    scale_ref, acc_ref, base_ref, past_ref, updated_hbm, velocity_hbm, updated_ref, velocity_ref, sems
):
    rate = outer_rate * (1.0 + outer_momentum)
    owned, _, width = acc_ref.shape
    part = owned // PARTS

    def copies(i):
        at = pl.ds(i * part, part)
        return [
            pltpu.make_async_copy(ref.at[at], hbm.at[at], sems.at[n, i])
            for n, (ref, hbm) in enumerate(
                ((updated_ref, updated_hbm), (velocity_ref, velocity_hbm))
            )
        ]

    for i in range(PARTS):

        def fill(m, _):
            scale = scale_ref[m][:, :1]
            for c in chunks(width):
                delta = scale * acc_ref[m, :, c]
                updated_ref[m, :, c] = base_ref[m, :, c] - rate * delta
                velocity_ref[m, :, c] = outer_momentum * past_ref[m, :, c] + delta
            return 0

        lax.fori_loop(i * part, (i + 1) * part, fill, 0)
        for copy in copies(i):
            copy.start()
    for i in range(PARTS):
        for copy in copies(i):
            copy.wait()


def unpack_kernel(order, places_ref, *rest):
    pieces, (out_ref, sems) = rest[:-2], rest[-2:]
    me = lax.axis_index("path").astype(jnp.int32)
    for wait in (False, True):
        for d, piece in zip(order, pieces, strict=True):
            for r in range(CAP):
                k = places_ref[(me ^ d) * CAP + r]

                @pl.when(k >= 0)
                def _():
                    copy = pltpu.make_async_copy(
                        piece.at[r], out_ref.at[0, k], sems.at[d * CAP + r]
                    )
                    if wait:
                        copy.wait()
                    else:
                        copy.start()


def on_device(path_params, global_params, momentum, module_ids, token_counts):
    paths, held = module_ids.shape
    owned, rows, width = global_params.shape
    shards = lax.axis_size("shard")
    module_ids, counts = in_hbm(module_ids, token_counts)
    slots = paths * CAP
    piece = pltpu.VMEM((CAP, rows, width), jnp.bfloat16)
    module = jax.ShapeDtypeStruct((owned, rows, width), jnp.float32)
    held_module = pltpu.VMEM(module.shape, module.dtype)
    tables = [
        pltpu.SMEM((paths * (CAP + 1),), jnp.int32),
        pltpu.SMEM((paths * (CAP + 1),), jnp.float32),
        pltpu.SMEM((owned,), jnp.float32),
    ]
    room = [
        pltpu.VMEM(module.shape, module.dtype),
        pltpu.VMEM(module.shape, module.dtype),
        pltpu.SemaphoreType.DMA((2, PARTS)),
    ]
    limits = pltpu.CompilerParams(vmem_limit_bytes=24 * 1024 * 1024)
    far = sorted(range(2, paths, 2), key=lambda d: (-d.bit_count(), d))
    order = far + [d + 1 for d in far[-1:] + far[:-1]] + [1]

    def exchange(pieces):
        return [
            lax.ppermute(x, "path", [(i, i ^ d) for i in range(paths)])
            for d, x in zip(order, pieces)
        ]

    places, *packed = pl.pallas_call(
        functools.partial(pack_kernel, owned, [*order, 0]),
        out_shape=[pltpu.SMEM((slots,), jnp.int32)] + [piece] * paths,
        in_specs=[ANY] * 2,
        out_specs=[SMEM] + [VMEM] * paths,
        scratch_shapes=[
            pltpu.SMEM(module_ids.shape, jnp.int32),
            pltpu.VMEM((held, rows, width), jnp.bfloat16),
            pltpu.SMEM((paths,), jnp.int32),
            pltpu.SemaphoreType.DMA((PARTS + 1,)),
        ],
        compiler_params=limits,
        name="pack",
    )(module_ids, *in_hbm(path_params.reshape(held, rows, width)))

    arrived = exchange(packed)
    table, weights, total, acc, base = pl.pallas_call(
        early_kernel,
        out_shape=tables + [held_module] * 2,
        in_specs=[SMEM] * 2 + [VMEM] + [ANY] * 2,
        out_specs=[SMEM] * 3 + [VMEM] * 2,
        scratch_shapes=room,
        compiler_params=limits,
        cost_estimate=pl.CostEstimate(flops=10**6, bytes_accessed=12 * 2**20, transcendentals=0),
        name="early",
    )(module_ids, counts, *in_vmem(packed[-1]), *in_hbm(global_params, momentum))
    acc, squares = pl.pallas_call(
        functools.partial(combine_kernel, order),
        out_shape=[held_module, jax.ShapeDtypeStruct((1, 128), jnp.float32)],
        in_specs=[SMEM] * 3 + [VMEM] * paths,
        out_specs=[VMEM] * 2,
        input_output_aliases={3: 0},
        compiler_params=limits,
        name="combine",
    )(*in_smem(table, weights, total), *in_vmem(acc, *arrived))
    parts = [squares] + [
        lax.ppermute(squares, "shard", [(i, (i + d) % shards) for i in range(shards)])
        for d in sorted(range(1, shards), key=lambda d: (d != 2, d))
    ]
    scale, *outgoing = pl.pallas_call(
        functools.partial(send_kernel, [*order, 0], shards),
        out_shape=[jax.ShapeDtypeStruct((owned, rows, 128), jnp.float32)] + [piece] * paths,
        in_specs=[SMEM] * 2 + [VMEM] * (2 + shards),
        out_specs=[VMEM] * (1 + paths),
        compiler_params=limits,
        name="send",
    )(*in_smem(table, total), *in_vmem(acc, base), *parts)
    returned = [*exchange(outgoing), outgoing[-1]]
    updated, velocity = pl.pallas_call(
        store_kernel,
        out_shape=[module] * 2,
        in_specs=[VMEM] * 4,
        out_specs=[ANY] * 2,
        scratch_shapes=room,
        compiler_params=limits,
        cost_estimate=pl.CostEstimate(flops=10**6, bytes_accessed=12 * 2**20, transcendentals=0),
        name="store",
    )(scale, *in_vmem(acc, base), momentum)
    path_out = pl.pallas_call(
        functools.partial(unpack_kernel, [*order, 0]),
        out_shape=jax.ShapeDtypeStruct(path_params.shape, path_params.dtype),
        in_specs=[SMEM] + [VMEM] * paths,
        out_specs=ANY,
        scratch_shapes=[pltpu.SemaphoreType.DMA((slots,))],
        name="unpack",
    )(*in_smem(places), *in_vmem(*returned))
    return updated, velocity, path_out


def solution(mesh):
    placed = (
        P("path", None, "shard", None),
        P("path", "shard", None),
        P("path", "shard", None),
        P(),
        P(),
    )
    return jax.shard_map(
        on_device,
        mesh=mesh,
        in_specs=placed,
        out_specs=(
            P("path", "shard", None),
            P("path", "shard", None),
            P("path", None, "shard", None),
        ),
        check_vma=False,
    )
```

```python
import functools

import jax
import jax.numpy as jnp
from jax import lax
from jax.experimental import pallas as pl
from jax.experimental.pallas import tpu as pltpu
from jax.sharding import PartitionSpec as P

CAP = 2
CHUNK = 1024
PARTS = 4
SOON = 2
outer_momentum = 0.9
outer_rate = 0.7

SMEM = pl.BlockSpec(memory_space=pltpu.SMEM)
VMEM = pl.BlockSpec(memory_space=pltpu.VMEM)
ANY = pl.BlockSpec(memory_space=pl.ANY)


def in_vmem(*arrays):
    return [pltpu.with_memory_space_constraint(x, pltpu.VMEM) for x in arrays]


def in_smem(*arrays):
    return [pltpu.with_memory_space_constraint(x, pltpu.SMEM) for x in arrays]


def in_hbm(*arrays):
    return [pltpu.with_memory_space_constraint(x, pltpu.HBM) for x in arrays]


def chunks(width):
    step = CHUNK if width % CHUNK == 0 else width
    return [pl.ds(at, step) for at in range(0, width, step)]


def pack_kernel(owned, order, ids_hbm, local_hbm, places_ref, *rest):
    pieces, (ids_ref, local_ref, seen, sems) = rest[:-4], rest[-4:]
    me = lax.axis_index("path").astype(jnp.int32)
    paths, held = ids_ref.shape
    parts = chunks(local_ref.shape[2])
    ids_copy = pltpu.make_async_copy(ids_hbm, ids_ref, sems.at[len(parts)])
    ids_copy.start()
    copies = [
        pltpu.make_async_copy(local_hbm.at[:, :, c], local_ref.at[:, :, c], sems.at[i])
        for i, c in enumerate(parts)
    ]
    for copy in copies:
        copy.start()
    for i in range(paths):
        seen[i] = jnp.int32(0)
    for i in range(paths * CAP):
        places_ref[i] = jnp.int32(-1)
    ids_copy.wait()
    for k in range(held):
        group = lax.div(ids_ref[me, k], jnp.int32(owned))
        rank = seen[group]
        seen[group] = rank + 1
        places_ref[group * CAP + rank] = jnp.int32(k)
    for c, copy in zip(parts, copies, strict=True):
        copy.wait()
        for d, piece in zip(order, pieces, strict=True):
            for r in range(CAP):
                k = jnp.maximum(places_ref[(me ^ d) * CAP + r], 0)
                piece[r, :, c] = local_ref[k, :, c]


def find_slots(me, owned, ids_ref, counts_ref, module_ref, weight_ref, total_ref):
    paths, held = ids_ref.shape

    def reset(i, _):
        total_ref[i] = jnp.float32(0.0)
        return 0

    def one(path, _):
        first = path * (CAP + 1)
        for r in range(CAP):
            module_ref[first + r] = jnp.int32(0)
            weight_ref[first + r] = jnp.float32(0.0)
        rank = jnp.int32(0)
        for k in range(held):
            at = ids_ref[path, k] - me * owned
            mine = (at >= 0) & (at < owned)
            slot = first + jnp.where(mine, rank, CAP)
            module_ref[slot] = at
            weight_ref[slot] = counts_ref[path, k].astype(jnp.float32)
            rank = rank + mine.astype(jnp.int32)
        for r in range(CAP):
            at = module_ref[first + r]
            total_ref[at] = total_ref[at] + weight_ref[first + r]
        return 0

    lax.fori_loop(0, owned, reset, 0)
    lax.fori_loop(0, paths, one, 0)


def subtract(me, pieces, distances, module_ref, weight_ref, acc_ref):
    width = acc_ref.shape[2]
    for piece, d in zip(pieces, distances, strict=True):
        for r in range(CAP):
            slot = (me ^ d) * (CAP + 1) + r
            m, weight = module_ref[slot], weight_ref[slot]
            for c in chunks(width):
                acc_ref[m, :, c] = acc_ref[m, :, c] - weight * piece[r, :, c].astype(jnp.float32)


def prepare(me, own_ref, params_hbm, past_hbm, tables, acc_ref, base_ref, params_ref, past_ref, sems, find):
    owned, _, width = acc_ref.shape
    part = owned // PARTS

    def copies(i):
        at = pl.ds(i * part, part)
        return [
            pltpu.make_async_copy(hbm.at[at], ref.at[at], sems.at[n, i])
            for n, (hbm, ref) in enumerate(((params_hbm, params_ref), (past_hbm, past_ref)))
        ]

    for i in range(PARTS):
        for copy in copies(i):
            copy.start()
    find()
    module_ref, weight_ref, total_ref = tables
    for i in range(PARTS):
        for copy in copies(i):
            copy.wait()

        def fill(m, _):
            for c in chunks(width):
                params = params_ref[m, :, c]
                acc_ref[m, :, c] = total_ref[m] * params
                base_ref[m, :, c] = params - (outer_rate * outer_momentum**2) * past_ref[m, :, c]
            return 0

        lax.fori_loop(i * part, (i + 1) * part, fill, 0)
    subtract(me, [own_ref], [0], module_ref, weight_ref, acc_ref)


def early_kernel(
    ids_ref, counts_ref, own_ref, params_hbm, past_hbm,
    module_ref, weight_ref, total_ref, acc_ref, base_ref, params_ref, past_ref, sems,
):
    me = lax.axis_index("path").astype(jnp.int32)
    tables = module_ref, weight_ref, total_ref
    find = functools.partial(find_slots, me, acc_ref.shape[0], ids_ref, counts_ref, *tables)
    prepare(
        me, own_ref, params_hbm, past_hbm, tables, acc_ref, base_ref, params_ref, past_ref, sems, find
    )


def diagonal(owned):
    row = lax.broadcasted_iota(jnp.int32, (owned, 128), 0)
    return row == lax.broadcasted_iota(jnp.int32, (owned, 128), 1)


def combine_kernel(order, module_ref, weight_ref, total_ref, acc_in, *rest):
    pieces, (acc_ref, squares_ref) = rest[:-2], rest[-2:]
    me = lax.axis_index("path").astype(jnp.int32)
    subtract(me, pieces, order, module_ref, weight_ref, acc_ref)
    owned, rows, width = acc_ref.shape
    sums = []
    for m in range(owned):
        inverse = 1.0 / jnp.maximum(jnp.full((rows, 128), total_ref[m], jnp.float32), 1.0)
        added = jnp.zeros((rows, 128), jnp.float32)
        for at in range(0, width, 128):
            raw = acc_ref[m, :, pl.ds(at, 128)] * inverse
            added = added + raw * raw
        sums.append(jnp.sum(added, axis=0, keepdims=True))
    sums = jnp.sum(jnp.concatenate(sums, axis=0), axis=1, keepdims=True)
    squares_ref[...] = jnp.sum(jnp.where(diagonal(owned), sums, 0.0), axis=0, keepdims=True)


def scales(entries, total, squares):
    inverse = 1.0 / jnp.maximum(total, 1.0)
    mean = jnp.sum(squares, axis=1, keepdims=True) / entries
    factor = jnp.minimum(1.0, 1.0 / jnp.sqrt(mean + 1e-06))
    return inverse * factor


def send_kernel(order, shards, module_ref, total_ref, acc_ref, base_ref, *rest):
    squares, (scale_ref, *pieces) = rest[:shards], rest[shards:]
    me = lax.axis_index("path").astype(jnp.int32)
    owned, rows, width = acc_ref.shape
    summed = squares[0][...]
    for other in squares[1:]:
        summed = summed + other[...]
    total = jnp.concatenate(
        [jnp.full((1, 128), total_ref[m], jnp.float32) for m in range(owned)], axis=0
    )
    summed = jnp.where(diagonal(owned), summed, 0.0)
    scale = scales(rows * width * shards, total, summed)
    for m in range(owned):
        scale_ref[m] = jnp.broadcast_to(scale[m : m + 1, :], (rows, 128))
    rate = outer_rate * (1.0 + outer_momentum)
    for d, piece in zip(order, pieces, strict=True):
        for r in range(CAP):
            m = module_ref[(me ^ d) * (CAP + 1) + r]
            step = rate * scale_ref[m][:, :1]
            for c in chunks(width):
                piece[r, :, c] = (base_ref[m, :, c] - step * acc_ref[m, :, c]).astype(
                    jnp.bfloat16
                )


def store_kernel(distances, places_ref, scale_ref, acc_ref, base_ref, past_ref, *rest):
    n = len(distances)
    pieces, (updated_hbm, velocity_hbm, out_hbm) = rest[:n], rest[n : n + 3]
    updated_ref, velocity_ref, sems, piece_sems = rest[n + 3 :]
    placed(distances, pieces, places_ref, out_hbm, piece_sems, start)
    rate = outer_rate * (1.0 + outer_momentum)
    owned, _, width = acc_ref.shape
    part = owned // PARTS

    def copies(i):
        at = pl.ds(i * part, part)
        return [
            pltpu.make_async_copy(ref.at[at], hbm.at[at], sems.at[n, i])
            for n, (ref, hbm) in enumerate(
                ((updated_ref, updated_hbm), (velocity_ref, velocity_hbm))
            )
        ]

    for i in range(PARTS):

        def fill(m, _):
            scale = scale_ref[m][:, :1]
            for c in chunks(width):
                delta = scale * acc_ref[m, :, c]
                updated_ref[m, :, c] = base_ref[m, :, c] - rate * delta
                velocity_ref[m, :, c] = outer_momentum * past_ref[m, :, c] + delta
            return 0

        lax.fori_loop(i * part, (i + 1) * part, fill, 0)
        for copy in copies(i):
            copy.start()
    for i in range(PARTS):
        for copy in copies(i):
            copy.wait()
    placed(distances, pieces, places_ref, out_hbm, piece_sems, wait)


def placed(distances, pieces, places_ref, out_ref, sems, act):
    me = lax.axis_index("path").astype(jnp.int32)
    for n, (d, piece) in enumerate(zip(distances, pieces, strict=True)):
        for r in range(CAP):
            k = places_ref[(me ^ d) * CAP + r]

            @pl.when(k >= 0)
            def _():
                act(pltpu.make_async_copy(piece.at[r], out_ref.at[0, k], sems.at[n * CAP + r]))


def start(copy):
    copy.start()


def wait(copy):
    copy.wait()


def unpack_kernel(distances, places_ref, *rest):
    pieces, (out_ref, sems) = rest[: len(distances)], rest[-2:]
    placed(distances, pieces, places_ref, out_ref, sems, start)
    placed(distances, pieces, places_ref, out_ref, sems, wait)


def on_device(path_params, global_params, momentum, module_ids, token_counts):
    paths, held = module_ids.shape
    owned, rows, width = global_params.shape
    shards = lax.axis_size("shard")
    module_ids, counts = in_hbm(module_ids, token_counts)
    slots = paths * CAP
    piece = pltpu.VMEM((CAP, rows, width), jnp.bfloat16)
    module = jax.ShapeDtypeStruct((owned, rows, width), jnp.float32)
    held_module = pltpu.VMEM(module.shape, module.dtype)
    tables = [
        pltpu.SMEM((paths * (CAP + 1),), jnp.int32),
        pltpu.SMEM((paths * (CAP + 1),), jnp.float32),
        pltpu.SMEM((owned,), jnp.float32),
    ]
    room = [
        pltpu.VMEM(module.shape, module.dtype),
        pltpu.VMEM(module.shape, module.dtype),
        pltpu.SemaphoreType.DMA((2, PARTS)),
    ]
    limits = pltpu.CompilerParams(vmem_limit_bytes=24 * 1024 * 1024)
    far = sorted(range(2, paths, 2), key=lambda d: (-d.bit_count(), d))
    there = far + [d + 1 for d in far[::-1]] + [1]
    back = far + [d + 1 for d in far[-1:] + far[:-1]] + [1]

    def exchange(order, pieces):
        return [
            lax.ppermute(x, "path", [(i, i ^ d) for i in range(paths)])
            for d, x in zip(order, pieces)
        ]

    places, *packed = pl.pallas_call(
        functools.partial(pack_kernel, owned, [*there, 0]),
        out_shape=[pltpu.SMEM((slots,), jnp.int32)] + [piece] * paths,
        in_specs=[ANY] * 2,
        out_specs=[SMEM] + [VMEM] * paths,
        scratch_shapes=[
            pltpu.SMEM(module_ids.shape, jnp.int32),
            pltpu.VMEM((held, rows, width), jnp.bfloat16),
            pltpu.SMEM((paths,), jnp.int32),
            pltpu.SemaphoreType.DMA((len(chunks(width)) + 1,)),
        ],
        compiler_params=limits,
        name="pack",
    )(module_ids, *in_hbm(path_params.reshape(held, rows, width)))

    arrived = exchange(there, packed)
    table, weights, total, acc, base = pl.pallas_call(
        early_kernel,
        out_shape=tables + [held_module] * 2,
        in_specs=[SMEM] * 2 + [VMEM] + [ANY] * 2,
        out_specs=[SMEM] * 3 + [VMEM] * 2,
        scratch_shapes=room,
        compiler_params=limits,
        cost_estimate=pl.CostEstimate(flops=10**6, bytes_accessed=12 * 2**20, transcendentals=0),
        name="early",
    )(module_ids, counts, *in_vmem(packed[-1]), *in_hbm(global_params, momentum))
    acc, squares = pl.pallas_call(
        functools.partial(combine_kernel, there),
        out_shape=[held_module, jax.ShapeDtypeStruct((1, 128), jnp.float32)],
        in_specs=[SMEM] * 3 + [VMEM] * paths,
        out_specs=[VMEM] * 2,
        input_output_aliases={3: 0},
        compiler_params=limits,
        name="combine",
    )(*in_smem(table, weights, total), *in_vmem(acc, *arrived))
    parts = [squares] + [
        lax.ppermute(squares, "shard", [(i, (i + d) % shards) for i in range(shards)])
        for d in sorted(range(1, shards), key=lambda d: (d == 2, -d))
    ]
    scale, *outgoing = pl.pallas_call(
        functools.partial(send_kernel, [*back, 0], shards),
        out_shape=[jax.ShapeDtypeStruct((owned, rows, 128), jnp.float32)] + [piece] * paths,
        in_specs=[SMEM] * 2 + [VMEM] * (2 + shards),
        out_specs=[VMEM] * (1 + paths),
        compiler_params=limits,
        name="send",
    )(*in_smem(table, total), *in_vmem(acc, base), *parts)
    returned = {0: outgoing[-1], **dict(zip(back, exchange(back, outgoing)))}
    soon, last = [0, *back[:SOON]], back[SOON:]
    whole = jax.ShapeDtypeStruct(path_params.shape, path_params.dtype)
    updated, velocity, path_out = pl.pallas_call(
        functools.partial(store_kernel, soon),
        out_shape=[module] * 2 + [whole],
        in_specs=[SMEM] + [VMEM] * (4 + len(soon)),
        out_specs=[ANY] * 3,
        scratch_shapes=room + [pltpu.SemaphoreType.DMA((len(soon) * CAP,))],
        compiler_params=limits,
        cost_estimate=pl.CostEstimate(flops=10**6, bytes_accessed=12 * 2**20, transcendentals=0),
        name="store",
    )(
        *in_smem(places), scale, *in_vmem(acc, base), momentum,
        *in_vmem(*[returned[d] for d in soon]),
    )
    path_out = pl.pallas_call(
        functools.partial(unpack_kernel, last),
        out_shape=whole,
        in_specs=[SMEM] + [VMEM] * len(last) + [ANY],
        out_specs=ANY,
        input_output_aliases={1 + len(last): 0},
        scratch_shapes=[pltpu.SemaphoreType.DMA((len(last) * CAP,))],
        name="unpack",
    )(*in_smem(places), *in_vmem(*[returned[d] for d in last]), path_out)
    return updated, velocity, path_out


def solution(mesh):
    placed = (
        P("path", None, "shard", None),
        P("path", "shard", None),
        P("path", "shard", None),
        P(),
        P(),
    )
    return jax.shard_map(
        on_device,
        mesh=mesh,
        in_specs=placed,
        out_specs=(
            P("path", "shard", None),
            P("path", "shard", None),
            P("path", None, "shard", None),
        ),
        check_vma=False,
    )
```

```python
import functools
import math

import jax
import jax.numpy as jnp
from jax import lax
from jax.experimental import pallas as pl
from jax.experimental.pallas import tpu as pltpu
from jax.sharding import PartitionSpec as P

CAP = 2
CHUNK = 1024
PARTS = 4
SOON = 2
outer_momentum = 0.9
outer_rate = 0.7

SMEM = pl.BlockSpec(memory_space=pltpu.SMEM)
VMEM = pl.BlockSpec(memory_space=pltpu.VMEM)
ANY = pl.BlockSpec(memory_space=pl.ANY)


def in_vmem(*arrays):
    return [pltpu.with_memory_space_constraint(x, pltpu.VMEM) for x in arrays]


def in_smem(*arrays):
    return [pltpu.with_memory_space_constraint(x, pltpu.SMEM) for x in arrays]


def in_hbm(*arrays):
    return [pltpu.with_memory_space_constraint(x, pltpu.HBM) for x in arrays]


def chunks(width):
    step = CHUNK if width % CHUNK == 0 else width
    return [pl.ds(at, step) for at in range(0, width, step)]


def pack_kernel(owned, order, ids_hbm, local_hbm, places_ref, *rest):
    pieces, (ids_ref, local_ref, seen, sems) = rest[:-4], rest[-4:]
    me = lax.axis_index("path").astype(jnp.int32)
    paths, held = ids_ref.shape
    parts = chunks(local_ref.shape[2])
    ids_copy = pltpu.make_async_copy(ids_hbm, ids_ref, sems.at[len(parts)])
    ids_copy.start()
    copies = [
        pltpu.make_async_copy(local_hbm.at[:, :, c], local_ref.at[:, :, c], sems.at[i])
        for i, c in enumerate(parts)
    ]
    for copy in copies:
        copy.start()
    for i in range(paths):
        seen[i] = jnp.int32(0)
    for i in range(paths * CAP):
        places_ref[i] = jnp.int32(-1)
    ids_copy.wait()
    for k in range(held):
        group = lax.div(ids_ref[me, k], jnp.int32(owned))
        rank = seen[group]
        seen[group] = rank + 1
        places_ref[group * CAP + rank] = jnp.int32(k)
    for c, copy in zip(parts, copies, strict=True):
        copy.wait()
        for d, piece in zip(order, pieces, strict=True):
            for r in range(CAP):
                k = jnp.maximum(places_ref[(me ^ d) * CAP + r], 0)
                piece[r, :, c] = local_ref[k, :, c]


def find_slots(me, owned, ids_ref, counts_ref, module_ref, weight_ref, total_ref):
    paths, held = ids_ref.shape

    def reset(i, _):
        total_ref[i] = jnp.float32(0.0)
        return 0

    def one(path, _):
        first = path * (CAP + 1)
        for r in range(CAP):
            module_ref[first + r] = jnp.int32(0)
            weight_ref[first + r] = jnp.float32(0.0)
        rank = jnp.int32(0)
        for k in range(held):
            at = ids_ref[path, k] - me * owned
            mine = (at >= 0) & (at < owned)
            slot = first + jnp.where(mine, rank, CAP)
            module_ref[slot] = at
            weight_ref[slot] = counts_ref[path, k].astype(jnp.float32)
            rank = rank + mine.astype(jnp.int32)
        for r in range(CAP):
            at = module_ref[first + r]
            total_ref[at] = total_ref[at] + weight_ref[first + r]
        return 0

    lax.fori_loop(0, owned, reset, 0)
    lax.fori_loop(0, paths, one, 0)


def subtract(me, pieces, distances, module_ref, weight_ref, acc_ref):
    width = acc_ref.shape[2]
    for piece, d in zip(pieces, distances, strict=True):
        for r in range(CAP):
            slot = (me ^ d) * (CAP + 1) + r
            m, weight = module_ref[slot], weight_ref[slot]
            for c in chunks(width):
                acc_ref[m, :, c] = acc_ref[m, :, c] - weight * piece[r, :, c].astype(jnp.float32)


def prepare(me, own_ref, params_hbm, past_hbm, tables, acc_ref, base_ref, params_ref, past_ref, sems, find):
    owned, _, width = acc_ref.shape
    parts = math.gcd(owned, PARTS)
    part = owned // parts

    def copies(i):
        at = pl.ds(i * part, part)
        return [
            pltpu.make_async_copy(hbm.at[at], ref.at[at], sems.at[n, i])
            for n, (hbm, ref) in enumerate(((params_hbm, params_ref), (past_hbm, past_ref)))
        ]

    for i in range(parts):
        for copy in copies(i):
            copy.start()
    find()
    module_ref, weight_ref, total_ref = tables
    for i in range(parts):
        for copy in copies(i):
            copy.wait()

        def fill(m, _):
            for c in chunks(width):
                params = params_ref[m, :, c]
                acc_ref[m, :, c] = total_ref[m] * params
                base_ref[m, :, c] = params - (outer_rate * outer_momentum**2) * past_ref[m, :, c]
            return 0

        lax.fori_loop(i * part, (i + 1) * part, fill, 0)
    subtract(me, [own_ref], [0], module_ref, weight_ref, acc_ref)


def early_kernel(
    ids_ref, counts_ref, own_ref, params_hbm, past_hbm,
    module_ref, weight_ref, total_ref, acc_ref, base_ref, params_ref, past_ref, sems,
):
    me = lax.axis_index("path").astype(jnp.int32)
    tables = module_ref, weight_ref, total_ref
    find = functools.partial(find_slots, me, acc_ref.shape[0], ids_ref, counts_ref, *tables)
    prepare(
        me, own_ref, params_hbm, past_hbm, tables, acc_ref, base_ref, params_ref, past_ref, sems, find
    )


def diagonal(owned):
    row = lax.broadcasted_iota(jnp.int32, (owned, 128), 0)
    return row == lax.broadcasted_iota(jnp.int32, (owned, 128), 1)


def combine_kernel(order, module_ref, weight_ref, total_ref, acc_in, *rest):
    pieces, (acc_ref, squares_ref) = rest[:-2], rest[-2:]
    me = lax.axis_index("path").astype(jnp.int32)
    subtract(me, pieces, order, module_ref, weight_ref, acc_ref)
    owned, rows, width = acc_ref.shape
    sums = []
    for m in range(owned):
        inverse = 1.0 / jnp.maximum(jnp.full((1, 128), total_ref[m], jnp.float32), 1.0)
        added = jnp.zeros((rows, 128), jnp.float32)
        for at in range(0, width, 128):
            acc = acc_ref[m, :, pl.ds(at, 128)]
            added = added + acc * acc
        sums.append(jnp.sum(added, axis=0, keepdims=True) * (inverse * inverse))
    sums = jnp.sum(jnp.concatenate(sums, axis=0), axis=1, keepdims=True)
    squares_ref[...] = jnp.sum(jnp.where(diagonal(owned), sums, 0.0), axis=0, keepdims=True)


def scales(entries, total, squares):
    inverse = 1.0 / jnp.maximum(total, 1.0)
    mean = jnp.sum(squares, axis=1, keepdims=True) / entries
    factor = jnp.minimum(1.0, 1.0 / jnp.sqrt(mean + 1e-06))
    return inverse * factor


def send_kernel(order, shards, module_ref, total_ref, acc_ref, base_ref, *rest):
    squares, (scale_ref, *pieces) = rest[:shards], rest[shards:]
    me = lax.axis_index("path").astype(jnp.int32)
    owned, rows, width = acc_ref.shape
    summed = squares[0][...]
    for other in squares[1:]:
        summed = summed + other[...]
    total = jnp.concatenate(
        [jnp.full((1, 128), total_ref[m], jnp.float32) for m in range(owned)], axis=0
    )
    summed = jnp.where(diagonal(owned), summed, 0.0)
    scale = scales(rows * width * shards, total, summed)
    for m in range(owned):
        scale_ref[m] = jnp.broadcast_to(scale[m : m + 1, :], (rows, 128))
    rate = outer_rate * (1.0 + outer_momentum)
    for d, piece in zip(order, pieces, strict=True):
        for r in range(CAP):
            m = module_ref[(me ^ d) * (CAP + 1) + r]
            step = rate * scale_ref[m][:, :1]
            for c in chunks(width):
                piece[r, :, c] = (base_ref[m, :, c] - step * acc_ref[m, :, c]).astype(
                    jnp.bfloat16
                )


def store_kernel(distances, places_ref, scale_ref, acc_ref, base_ref, past_ref, *rest):
    n = len(distances)
    pieces, (updated_hbm, velocity_hbm, out_hbm) = rest[:n], rest[n : n + 3]
    updated_ref, velocity_ref, sems, piece_sems = rest[n + 3 :]
    placed(distances, pieces, places_ref, out_hbm, piece_sems, start)
    rate = outer_rate * (1.0 + outer_momentum)
    owned, _, width = acc_ref.shape
    parts = math.gcd(owned, PARTS)
    part = owned // parts

    def copies(i):
        at = pl.ds(i * part, part)
        return [
            pltpu.make_async_copy(ref.at[at], hbm.at[at], sems.at[n, i])
            for n, (ref, hbm) in enumerate(
                ((updated_ref, updated_hbm), (velocity_ref, velocity_hbm))
            )
        ]

    for i in range(parts):

        def fill(m, _):
            scale = scale_ref[m][:, :1]
            for c in chunks(width):
                delta = scale * acc_ref[m, :, c]
                updated_ref[m, :, c] = base_ref[m, :, c] - rate * delta
                velocity_ref[m, :, c] = outer_momentum * past_ref[m, :, c] + delta
            return 0

        lax.fori_loop(i * part, (i + 1) * part, fill, 0)
        for copy in copies(i):
            copy.start()
    for i in range(parts):
        for copy in copies(i):
            copy.wait()
    placed(distances, pieces, places_ref, out_hbm, piece_sems, wait)


def placed(distances, pieces, places_ref, out_ref, sems, act):
    me = lax.axis_index("path").astype(jnp.int32)
    for n, (d, piece) in enumerate(zip(distances, pieces, strict=True)):
        for r in range(CAP):
            k = places_ref[(me ^ d) * CAP + r]

            @pl.when(k >= 0)
            def _():
                act(pltpu.make_async_copy(piece.at[r], out_ref.at[0, k], sems.at[n * CAP + r]))


def start(copy):
    copy.start()


def wait(copy):
    copy.wait()


def unpack_kernel(distances, places_ref, *rest):
    pieces, (out_ref, sems) = rest[: len(distances)], rest[-2:]
    placed(distances, pieces, places_ref, out_ref, sems, start)
    placed(distances, pieces, places_ref, out_ref, sems, wait)


def on_device(path_params, global_params, momentum, module_ids, token_counts):
    paths, held = module_ids.shape
    owned, rows, width = global_params.shape
    shards = lax.axis_size("shard")
    module_ids, counts = in_hbm(module_ids, token_counts)
    slots = paths * CAP
    piece = pltpu.VMEM((CAP, rows, width), jnp.bfloat16)
    module = jax.ShapeDtypeStruct((owned, rows, width), jnp.float32)
    held_module = pltpu.VMEM(module.shape, module.dtype)
    tables = [
        pltpu.SMEM((paths * (CAP + 1),), jnp.int32),
        pltpu.SMEM((paths * (CAP + 1),), jnp.float32),
        pltpu.SMEM((owned,), jnp.float32),
    ]
    room = [
        pltpu.VMEM(module.shape, module.dtype),
        pltpu.VMEM(module.shape, module.dtype),
        pltpu.SemaphoreType.DMA((2, PARTS)),
    ]
    limits = pltpu.CompilerParams(vmem_limit_bytes=24 * 1024 * 1024)
    far = sorted(range(2, paths, 2), key=lambda d: (-d.bit_count(), d))
    there = far + [d + 1 for d in far[::-1]] + [1]
    back = far + [d + 1 for d in far[-1:] + far[:-1]] + [1]

    def exchange(order, pieces):
        return [
            lax.ppermute(x, "path", [(i, i ^ d) for i in range(paths)])
            for d, x in zip(order, pieces)
        ]

    places, *packed = pl.pallas_call(
        functools.partial(pack_kernel, owned, [*there, 0]),
        out_shape=[pltpu.SMEM((slots,), jnp.int32)] + [piece] * paths,
        in_specs=[ANY] * 2,
        out_specs=[SMEM] + [VMEM] * paths,
        scratch_shapes=[
            pltpu.SMEM(module_ids.shape, jnp.int32),
            pltpu.VMEM((held, rows, width), jnp.bfloat16),
            pltpu.SMEM((paths,), jnp.int32),
            pltpu.SemaphoreType.DMA((len(chunks(width)) + 1,)),
        ],
        compiler_params=limits,
        name="pack",
    )(module_ids, *in_hbm(path_params.reshape(held, rows, width)))

    arrived = exchange(there, packed)
    table, weights, total, acc, base = pl.pallas_call(
        early_kernel,
        out_shape=tables + [held_module] * 2,
        in_specs=[SMEM] * 2 + [VMEM] + [ANY] * 2,
        out_specs=[SMEM] * 3 + [VMEM] * 2,
        scratch_shapes=room,
        compiler_params=limits,
        cost_estimate=pl.CostEstimate(flops=10**6, bytes_accessed=12 * 2**20, transcendentals=0),
        name="early",
    )(module_ids, counts, *in_vmem(packed[-1]), *in_hbm(global_params, momentum))
    acc, squares = pl.pallas_call(
        functools.partial(combine_kernel, there),
        out_shape=[held_module, jax.ShapeDtypeStruct((1, 128), jnp.float32)],
        in_specs=[SMEM] * 3 + [VMEM] * paths,
        out_specs=[VMEM] * 2,
        input_output_aliases={3: 0},
        compiler_params=limits,
        name="combine",
    )(*in_smem(table, weights, total), *in_vmem(acc, *arrived))
    parts = [squares] + [
        lax.ppermute(squares, "shard", [(i, (i + d) % shards) for i in range(shards)])
        for d in sorted(range(1, shards), key=lambda d: (d == 2, -d))
    ]
    scale, *outgoing = pl.pallas_call(
        functools.partial(send_kernel, [*back, 0], shards),
        out_shape=[jax.ShapeDtypeStruct((owned, rows, 128), jnp.float32)] + [piece] * paths,
        in_specs=[SMEM] * 2 + [VMEM] * (2 + shards),
        out_specs=[VMEM] * (1 + paths),
        compiler_params=limits,
        name="send",
    )(*in_smem(table, total), *in_vmem(acc, base), *parts)
    returned = {0: outgoing[-1], **dict(zip(back, exchange(back, outgoing)))}
    soon, last = [0, *back[:SOON]], back[SOON:]
    whole = jax.ShapeDtypeStruct(path_params.shape, path_params.dtype)
    updated, velocity, path_out = pl.pallas_call(
        functools.partial(store_kernel, soon),
        out_shape=[module] * 2 + [whole],
        in_specs=[SMEM] + [VMEM] * (4 + len(soon)),
        out_specs=[ANY] * 3,
        scratch_shapes=room + [pltpu.SemaphoreType.DMA((len(soon) * CAP,))],
        compiler_params=limits,
        cost_estimate=pl.CostEstimate(flops=10**6, bytes_accessed=12 * 2**20, transcendentals=0),
        name="store",
    )(
        *in_smem(places), scale, *in_vmem(acc, base), momentum,
        *in_vmem(*[returned[d] for d in soon]),
    )
    path_out = pl.pallas_call(
        functools.partial(unpack_kernel, last),
        out_shape=whole,
        in_specs=[SMEM] + [VMEM] * len(last) + [ANY],
        out_specs=ANY,
        input_output_aliases={1 + len(last): 0},
        scratch_shapes=[pltpu.SemaphoreType.DMA((len(last) * CAP,))],
        name="unpack",
    )(*in_smem(places), *in_vmem(*[returned[d] for d in last]), path_out)
    return updated, velocity, path_out


def solution(mesh):
    placed = (
        P("path", None, "shard", None),
        P("path", "shard", None),
        P("path", "shard", None),
        P(),
        P(),
    )
    return jax.shard_map(
        on_device,
        mesh=mesh,
        in_specs=placed,
        out_specs=(
            P("path", "shard", None),
            P("path", "shard", None),
            P("path", None, "shard", None),
        ),
        check_vma=False,
    )
```

```python
import functools
import math

import jax
import jax.numpy as jnp
from jax import lax
from jax.experimental import pallas as pl
from jax.experimental.pallas import tpu as pltpu
from jax.sharding import PartitionSpec as P

CAP = 2
CHUNK = 1024
PARTS = 4
SOON = 2
AHEAD = 3
outer_momentum = 0.9
outer_rate = 0.7

SMEM = pl.BlockSpec(memory_space=pltpu.SMEM)
VMEM = pl.BlockSpec(memory_space=pltpu.VMEM)
ANY = pl.BlockSpec(memory_space=pl.ANY)


def in_vmem(*arrays):
    return [pltpu.with_memory_space_constraint(x, pltpu.VMEM) for x in arrays]


def in_smem(*arrays):
    return [pltpu.with_memory_space_constraint(x, pltpu.SMEM) for x in arrays]


def in_hbm(*arrays):
    return [pltpu.with_memory_space_constraint(x, pltpu.HBM) for x in arrays]


def chunks(width):
    step = CHUNK if width % CHUNK == 0 else width
    return [pl.ds(at, step) for at in range(0, width, step)]


def pack_kernel(owned, order, ids_hbm, local_hbm, places_ref, *rest):
    pieces, (ids_ref, local_ref, seen, sems) = rest[:-4], rest[-4:]
    me = lax.axis_index("path").astype(jnp.int32)
    paths, held = ids_ref.shape
    parts = chunks(local_ref.shape[2])
    ids_copy = pltpu.make_async_copy(ids_hbm, ids_ref, sems.at[len(parts)])
    ids_copy.start()
    copies = [
        pltpu.make_async_copy(local_hbm.at[:, :, c], local_ref.at[:, :, c], sems.at[i])
        for i, c in enumerate(parts)
    ]
    for copy in copies:
        copy.start()
    for i in range(paths):
        seen[i] = jnp.int32(0)
    for i in range(paths * CAP):
        places_ref[i] = jnp.int32(-1)
    ids_copy.wait()
    for k in range(held):
        group = lax.div(ids_ref[me, k], jnp.int32(owned))
        rank = seen[group]
        seen[group] = rank + 1
        places_ref[group * CAP + rank] = jnp.int32(k)
    for c, copy in zip(parts, copies, strict=True):
        copy.wait()
        for d, piece in zip(order, pieces, strict=True):
            for r in range(CAP):
                k = jnp.maximum(places_ref[(me ^ d) * CAP + r], 0)
                piece[r, :, c] = local_ref[k, :, c]


def find_slots(me, owned, ids_ref, counts_ref, module_ref, weight_ref, total_ref):
    paths, held = ids_ref.shape

    def reset(i, _):
        total_ref[i] = jnp.float32(0.0)
        return 0

    def one(path, _):
        first = path * (CAP + 1)
        for r in range(CAP):
            module_ref[first + r] = jnp.int32(0)
            weight_ref[first + r] = jnp.float32(0.0)
        rank = jnp.int32(0)
        for k in range(held):
            at = ids_ref[path, k] - me * owned
            mine = (at >= 0) & (at < owned)
            slot = first + jnp.where(mine, rank, CAP)
            module_ref[slot] = at
            weight_ref[slot] = counts_ref[path, k].astype(jnp.float32)
            rank = rank + mine.astype(jnp.int32)
        for r in range(CAP):
            at = module_ref[first + r]
            total_ref[at] = total_ref[at] + weight_ref[first + r]
        return 0

    lax.fori_loop(0, owned, reset, 0)
    lax.fori_loop(0, paths, one, 0)


def subtract(me, pieces, distances, module_ref, weight_ref, acc_ref):
    width = acc_ref.shape[2]
    for piece, d in zip(pieces, distances, strict=True):
        for r in range(CAP):
            slot = (me ^ d) * (CAP + 1) + r
            m, weight = module_ref[slot], weight_ref[slot]
            for c in chunks(width):
                acc_ref[m, :, c] = acc_ref[m, :, c] - weight * piece[r, :, c].astype(jnp.float32)


def prepare(me, own_ref, params_hbm, past_hbm, tables, acc_ref, base_ref, params_ref, past_ref, sems, find):
    owned, _, width = acc_ref.shape
    parts = math.gcd(owned, PARTS)
    part = owned // parts

    def copies(i):
        at = pl.ds(i * part, part)
        return [
            pltpu.make_async_copy(hbm.at[at], ref.at[at], sems.at[n, i])
            for n, (hbm, ref) in enumerate(((params_hbm, params_ref), (past_hbm, past_ref)))
        ]

    for i in range(parts):
        for copy in copies(i):
            copy.start()
    find()
    module_ref, weight_ref, total_ref = tables
    for i in range(parts):
        for copy in copies(i):
            copy.wait()

        def fill(m, _):
            for c in chunks(width):
                params = params_ref[m, :, c]
                acc_ref[m, :, c] = total_ref[m] * params
                base_ref[m, :, c] = params - (outer_rate * outer_momentum**2) * past_ref[m, :, c]
            return 0

        lax.fori_loop(i * part, (i + 1) * part, fill, 0)
    subtract(me, [own_ref], [0], module_ref, weight_ref, acc_ref)


def early_kernel(
    ids_ref, counts_ref, own_ref, params_hbm, past_hbm,
    module_ref, weight_ref, total_ref, acc_ref, base_ref, params_ref, past_ref, sems,
):
    me = lax.axis_index("path").astype(jnp.int32)
    tables = module_ref, weight_ref, total_ref
    find = functools.partial(find_slots, me, acc_ref.shape[0], ids_ref, counts_ref, *tables)
    prepare(
        me, own_ref, params_hbm, past_hbm, tables, acc_ref, base_ref, params_ref, past_ref, sems, find
    )


def diagonal(owned):
    row = lax.broadcasted_iota(jnp.int32, (owned, 128), 0)
    return row == lax.broadcasted_iota(jnp.int32, (owned, 128), 1)


def combine_kernel(order, module_ref, weight_ref, total_ref, acc_in, *rest):
    pieces, (acc_ref, squares_ref) = rest[:-2], rest[-2:]
    me = lax.axis_index("path").astype(jnp.int32)
    subtract(me, pieces, order, module_ref, weight_ref, acc_ref)
    owned, rows, width = acc_ref.shape
    sums = []
    for m in range(owned):
        inverse = 1.0 / jnp.maximum(jnp.full((1, 128), total_ref[m], jnp.float32), 1.0)
        added = jnp.zeros((rows, 128), jnp.float32)
        for at in range(0, width, 128):
            acc = acc_ref[m, :, pl.ds(at, 128)]
            added = added + acc * acc
        sums.append(jnp.sum(added, axis=0, keepdims=True) * (inverse * inverse))
    sums = jnp.sum(jnp.concatenate(sums, axis=0), axis=1, keepdims=True)
    squares_ref[...] = jnp.sum(jnp.where(diagonal(owned), sums, 0.0), axis=0, keepdims=True)


def scales(entries, total, squares):
    inverse = 1.0 / jnp.maximum(total, 1.0)
    mean = jnp.sum(squares, axis=1, keepdims=True) / entries
    factor = jnp.minimum(1.0, 1.0 / jnp.sqrt(mean + 1e-06))
    return inverse * factor


def send_kernel(order, shards, module_ref, total_ref, acc_ref, base_ref, *rest):
    squares, (scale_ref, *pieces) = rest[:shards], rest[shards:]
    me = lax.axis_index("path").astype(jnp.int32)
    owned, rows, width = acc_ref.shape
    summed = squares[0][...]
    for other in squares[1:]:
        summed = summed + other[...]
    total = jnp.concatenate(
        [jnp.full((1, 128), total_ref[m], jnp.float32) for m in range(owned)], axis=0
    )
    summed = jnp.where(diagonal(owned), summed, 0.0)
    scale = scales(rows * width * shards, total, summed)
    for m in range(owned):
        scale_ref[m] = jnp.broadcast_to(scale[m : m + 1, :], (rows, 128))
    rate = outer_rate * (1.0 + outer_momentum)
    for d, piece in zip(order, pieces, strict=True):
        for r in range(CAP):
            m = module_ref[(me ^ d) * (CAP + 1) + r]
            step = rate * scale_ref[m][:, :1]
            for c in chunks(width):
                piece[r, :, c] = (base_ref[m, :, c] - step * acc_ref[m, :, c]).astype(
                    jnp.bfloat16
                )


def store_kernel(distances, places_ref, scale_ref, acc_ref, base_ref, past_ref, *rest):
    n = len(distances)
    pieces, (updated_hbm, velocity_hbm, out_hbm) = rest[:n], rest[n : n + 3]
    updated_ref, velocity_ref, sems, piece_sems = rest[n + 3 :]
    placed(distances, pieces, places_ref, out_hbm, piece_sems, start)
    rate = outer_rate * (1.0 + outer_momentum)
    owned, _, width = acc_ref.shape
    parts = math.gcd(owned, PARTS)
    part = owned // parts

    def copies(i):
        at = pl.ds(i * part, part)
        return [
            pltpu.make_async_copy(ref.at[at], hbm.at[at], sems.at[n, i])
            for n, (ref, hbm) in enumerate(
                ((updated_ref, updated_hbm), (velocity_ref, velocity_hbm))
            )
        ]

    for i in range(parts):

        def fill(m, _):
            scale = scale_ref[m][:, :1]
            for c in chunks(width):
                delta = scale * acc_ref[m, :, c]
                updated_ref[m, :, c] = base_ref[m, :, c] - rate * delta
                velocity_ref[m, :, c] = outer_momentum * past_ref[m, :, c] + delta
            return 0

        lax.fori_loop(i * part, (i + 1) * part, fill, 0)
        for copy in copies(i):
            copy.start()
    for i in range(parts):
        for copy in copies(i):
            copy.wait()
    placed(distances, pieces, places_ref, out_hbm, piece_sems, wait)


def placed(distances, pieces, places_ref, out_ref, sems, act):
    me = lax.axis_index("path").astype(jnp.int32)
    for n, (d, piece) in enumerate(zip(distances, pieces, strict=True)):
        for r in range(CAP):
            k = places_ref[(me ^ d) * CAP + r]

            @pl.when(k >= 0)
            def _():
                act(pltpu.make_async_copy(piece.at[r], out_ref.at[0, k], sems.at[n * CAP + r]))


def start(copy):
    copy.start()


def wait(copy):
    copy.wait()


def unpack_kernel(distances, places_ref, *rest):
    pieces, (out_ref, sems) = rest[: len(distances)], rest[-2:]
    placed(distances, pieces, places_ref, out_ref, sems, start)
    placed(distances, pieces, places_ref, out_ref, sems, wait)


def on_device(path_params, global_params, momentum, module_ids, token_counts):
    paths, held = module_ids.shape
    owned, rows, width = global_params.shape
    shards = lax.axis_size("shard")
    module_ids, counts = in_hbm(module_ids, token_counts)
    slots = paths * CAP
    piece = pltpu.VMEM((CAP, rows, width), jnp.bfloat16)
    module = jax.ShapeDtypeStruct((owned, rows, width), jnp.float32)
    held_module = pltpu.VMEM(module.shape, module.dtype)
    tables = [
        pltpu.SMEM((paths * (CAP + 1),), jnp.int32),
        pltpu.SMEM((paths * (CAP + 1),), jnp.float32),
        pltpu.SMEM((owned,), jnp.float32),
    ]
    room = [
        pltpu.VMEM(module.shape, module.dtype),
        pltpu.VMEM(module.shape, module.dtype),
        pltpu.SemaphoreType.DMA((2, PARTS)),
    ]
    limits = pltpu.CompilerParams(vmem_limit_bytes=24 * 1024 * 1024)
    far = sorted(range(2, paths, 2), key=lambda d: (-d.bit_count(), d))
    there = far + [d + 1 for d in far[::-1]] + [1]
    back = far + [d + 1 for d in far[-1:] + far[:-1]] + [1]

    def exchange(order, pieces):
        return [
            lax.ppermute(x, "path", [(i, i ^ d) for i in range(paths)])
            for d, x in zip(order, pieces)
        ]

    (local,) = in_hbm(path_params.reshape(held, rows, width))

    def pack(distances):
        return pl.pallas_call(
            functools.partial(pack_kernel, owned, distances),
            out_shape=[pltpu.SMEM((slots,), jnp.int32)] + [piece] * len(distances),
            in_specs=[ANY] * 2,
            out_specs=[SMEM] + [VMEM] * len(distances),
            scratch_shapes=[
                pltpu.SMEM(module_ids.shape, jnp.int32),
                pltpu.VMEM((held, rows, width), jnp.bfloat16),
                pltpu.SMEM((paths,), jnp.int32),
                pltpu.SemaphoreType.DMA((len(chunks(width)) + 1,)),
            ],
            compiler_params=limits,
            name="pack",
        )(module_ids, local)

    places, *packed = pack(there[:AHEAD])
    packed += pack([*there[AHEAD:], 0])[1:]
    arrived = exchange(there, packed)
    table, weights, total, acc, base = pl.pallas_call(
        early_kernel,
        out_shape=tables + [held_module] * 2,
        in_specs=[SMEM] * 2 + [VMEM] + [ANY] * 2,
        out_specs=[SMEM] * 3 + [VMEM] * 2,
        scratch_shapes=room,
        compiler_params=limits,
        cost_estimate=pl.CostEstimate(flops=10**6, bytes_accessed=12 * 2**20, transcendentals=0),
        name="early",
    )(module_ids, counts, *in_vmem(packed[-1]), *in_hbm(global_params, momentum))
    acc, squares = pl.pallas_call(
        functools.partial(combine_kernel, there),
        out_shape=[held_module, jax.ShapeDtypeStruct((1, 128), jnp.float32)],
        in_specs=[SMEM] * 3 + [VMEM] * paths,
        out_specs=[VMEM] * 2,
        input_output_aliases={3: 0},
        compiler_params=limits,
        name="combine",
    )(*in_smem(table, weights, total), *in_vmem(acc, *arrived))
    parts = [squares] + [
        lax.ppermute(squares, "shard", [(i, (i + d) % shards) for i in range(shards)])
        for d in sorted(range(1, shards), key=lambda d: (d == 2, -d))
    ]
    def send(distances):
        return pl.pallas_call(
            functools.partial(send_kernel, distances, shards),
            out_shape=[jax.ShapeDtypeStruct((owned, rows, 128), jnp.float32)]
            + [piece] * len(distances),
            in_specs=[SMEM] * 2 + [VMEM] * (2 + shards),
            out_specs=[VMEM] * (1 + len(distances)),
            compiler_params=limits,
            name="send",
        )(*in_smem(table, total), *in_vmem(acc, base), *parts)

    scale, *outgoing = send([*back, 0])
    returned = {0: outgoing[-1], **dict(zip(back, exchange(back, outgoing)))}
    soon, last = [0, *back[:SOON]], back[SOON:]
    whole = jax.ShapeDtypeStruct(path_params.shape, path_params.dtype)
    updated, velocity, path_out = pl.pallas_call(
        functools.partial(store_kernel, soon),
        out_shape=[module] * 2 + [whole],
        in_specs=[SMEM] + [VMEM] * (4 + len(soon)),
        out_specs=[ANY] * 3,
        scratch_shapes=room + [pltpu.SemaphoreType.DMA((len(soon) * CAP,))],
        compiler_params=limits,
        cost_estimate=pl.CostEstimate(flops=10**6, bytes_accessed=12 * 2**20, transcendentals=0),
        name="store",
    )(
        *in_smem(places), scale, *in_vmem(acc, base), momentum,
        *in_vmem(*[returned[d] for d in soon]),
    )
    path_out = pl.pallas_call(
        functools.partial(unpack_kernel, last),
        out_shape=whole,
        in_specs=[SMEM] + [VMEM] * len(last) + [ANY],
        out_specs=ANY,
        input_output_aliases={1 + len(last): 0},
        scratch_shapes=[pltpu.SemaphoreType.DMA((len(last) * CAP,))],
        name="unpack",
    )(*in_smem(places), *in_vmem(*[returned[d] for d in last]), path_out)
    return updated, velocity, path_out


def solution(mesh):
    placed = (
        P("path", None, "shard", None),
        P("path", "shard", None),
        P("path", "shard", None),
        P(),
        P(),
    )
    return jax.shard_map(
        on_device,
        mesh=mesh,
        in_specs=placed,
        out_specs=(
            P("path", "shard", None),
            P("path", "shard", None),
            P("path", None, "shard", None),
        ),
        check_vma=False,
    )
```

```python
import functools
import math

import jax
import jax.numpy as jnp
from jax import lax
from jax.experimental import pallas as pl
from jax.experimental.pallas import tpu as pltpu
from jax.sharding import PartitionSpec as P

CAP = 2
CHUNK = 2048
PARTS = 4
SOON = 2
outer_momentum = 0.9
outer_rate = 0.7

SMEM = pl.BlockSpec(memory_space=pltpu.SMEM)
VMEM = pl.BlockSpec(memory_space=pltpu.VMEM)
ANY = pl.BlockSpec(memory_space=pl.ANY)


def in_vmem(*arrays):
    return [pltpu.with_memory_space_constraint(x, pltpu.VMEM) for x in arrays]


def in_smem(*arrays):
    return [pltpu.with_memory_space_constraint(x, pltpu.SMEM) for x in arrays]


def in_hbm(*arrays):
    return [pltpu.with_memory_space_constraint(x, pltpu.HBM) for x in arrays]


def chunks(width):
    step = CHUNK if width % CHUNK == 0 else width
    return [pl.ds(at, step) for at in range(0, width, step)]


def pack_kernel(owned, order, ids_hbm, local_hbm, places_ref, *rest):
    pieces, (ids_ref, local_ref, seen, sems) = rest[:-4], rest[-4:]
    me = lax.axis_index("path").astype(jnp.int32)
    paths, held = ids_ref.shape
    parts = chunks(local_ref.shape[2])
    ids_copy = pltpu.make_async_copy(ids_hbm, ids_ref, sems.at[len(parts)])
    ids_copy.start()
    copies = [
        pltpu.make_async_copy(local_hbm.at[:, :, c], local_ref.at[:, :, c], sems.at[i])
        for i, c in enumerate(parts)
    ]
    for copy in copies:
        copy.start()
    for i in range(paths):
        seen[i] = jnp.int32(0)
    for i in range(paths * CAP):
        places_ref[i] = jnp.int32(-1)
    ids_copy.wait()
    for k in range(held):
        group = lax.div(ids_ref[me, k], jnp.int32(owned))
        rank = seen[group]
        seen[group] = rank + 1
        places_ref[group * CAP + rank] = jnp.int32(k)
    for c, copy in zip(parts, copies, strict=True):
        copy.wait()
        for d, piece in zip(order, pieces, strict=True):
            for r in range(CAP):
                k = jnp.maximum(places_ref[(me ^ d) * CAP + r], 0)
                piece[r, :, c] = local_ref[k, :, c]


def find_slots(me, owned, ids_ref, counts_ref, module_ref, weight_ref, total_ref):
    paths, held = ids_ref.shape

    def reset(i, _):
        total_ref[i] = jnp.float32(0.0)
        return 0

    def one(path, _):
        first = path * (CAP + 1)
        for r in range(CAP):
            module_ref[first + r] = jnp.int32(0)
            weight_ref[first + r] = jnp.float32(0.0)
        rank = jnp.int32(0)
        for k in range(held):
            at = ids_ref[path, k] - me * owned
            mine = (at >= 0) & (at < owned)
            slot = first + jnp.where(mine, rank, CAP)
            module_ref[slot] = at
            weight_ref[slot] = counts_ref[path, k].astype(jnp.float32)
            rank = rank + mine.astype(jnp.int32)
        for r in range(CAP):
            at = module_ref[first + r]
            total_ref[at] = total_ref[at] + weight_ref[first + r]
        return 0

    lax.fori_loop(0, owned, reset, 0)
    lax.fori_loop(0, paths, one, 0)


def subtract(me, pieces, distances, module_ref, weight_ref, acc_ref):
    width = acc_ref.shape[2]
    for piece, d in zip(pieces, distances, strict=True):
        for r in range(CAP):
            slot = (me ^ d) * (CAP + 1) + r
            m, weight = module_ref[slot], weight_ref[slot]
            for c in chunks(width):
                acc_ref[m, :, c] = acc_ref[m, :, c] - weight * piece[r, :, c].astype(jnp.float32)


def prepare(me, own_ref, params_hbm, past_hbm, tables, acc_ref, base_ref, params_ref, past_ref, sems, find):
    owned, _, width = acc_ref.shape
    parts = math.gcd(owned, PARTS)
    part = owned // parts

    def copies(i):
        at = pl.ds(i * part, part)
        return [
            pltpu.make_async_copy(hbm.at[at], ref.at[at], sems.at[n, i])
            for n, (hbm, ref) in enumerate(((params_hbm, params_ref), (past_hbm, past_ref)))
        ]

    for i in range(parts):
        for copy in copies(i):
            copy.start()
    find()
    module_ref, weight_ref, total_ref = tables
    for i in range(parts):
        for copy in copies(i):
            copy.wait()

        def fill(m, _):
            for c in chunks(width):
                params = params_ref[m, :, c]
                acc_ref[m, :, c] = total_ref[m] * params
                base_ref[m, :, c] = params - (outer_rate * outer_momentum**2) * past_ref[m, :, c]
            return 0

        lax.fori_loop(i * part, (i + 1) * part, fill, 0)
    subtract(me, [own_ref], [0], module_ref, weight_ref, acc_ref)


def early_kernel(
    ids_ref, counts_ref, own_ref, params_hbm, past_hbm,
    module_ref, weight_ref, total_ref, acc_ref, base_ref, params_ref, past_ref, sems,
):
    me = lax.axis_index("path").astype(jnp.int32)
    tables = module_ref, weight_ref, total_ref
    find = functools.partial(find_slots, me, acc_ref.shape[0], ids_ref, counts_ref, *tables)
    prepare(
        me, own_ref, params_hbm, past_hbm, tables, acc_ref, base_ref, params_ref, past_ref, sems, find
    )


def diagonal(owned):
    row = lax.broadcasted_iota(jnp.int32, (owned, 128), 0)
    return row == lax.broadcasted_iota(jnp.int32, (owned, 128), 1)


def combine_kernel(order, module_ref, weight_ref, total_ref, acc_in, *rest):
    pieces, (acc_ref, squares_ref) = rest[:-2], rest[-2:]
    me = lax.axis_index("path").astype(jnp.int32)
    subtract(me, pieces, order, module_ref, weight_ref, acc_ref)
    owned, rows, width = acc_ref.shape
    sums = []
    for m in range(owned):
        inverse = 1.0 / jnp.maximum(jnp.full((1, 128), total_ref[m], jnp.float32), 1.0)
        added = jnp.zeros((rows, 128), jnp.float32)
        for at in range(0, width, 128):
            acc = acc_ref[m, :, pl.ds(at, 128)]
            added = added + acc * acc
        sums.append(jnp.sum(added, axis=0, keepdims=True) * (inverse * inverse))
    sums = jnp.sum(jnp.concatenate(sums, axis=0), axis=1, keepdims=True)
    squares_ref[...] = jnp.sum(jnp.where(diagonal(owned), sums, 0.0), axis=0, keepdims=True)


def scales(entries, total, squares):
    inverse = 1.0 / jnp.maximum(total, 1.0)
    mean = jnp.sum(squares, axis=1, keepdims=True) / entries
    factor = jnp.minimum(1.0, 1.0 / jnp.sqrt(mean + 1e-06))
    return inverse * factor


def send_kernel(order, shards, module_ref, total_ref, acc_ref, base_ref, *rest):
    squares, (scale_ref, *pieces) = rest[:shards], rest[shards:]
    me = lax.axis_index("path").astype(jnp.int32)
    owned, rows, width = acc_ref.shape
    summed = squares[0][...]
    for other in squares[1:]:
        summed = summed + other[...]
    total = jnp.concatenate(
        [jnp.full((1, 128), total_ref[m], jnp.float32) for m in range(owned)], axis=0
    )
    summed = jnp.where(diagonal(owned), summed, 0.0)
    scale = scales(rows * width * shards, total, summed)
    for m in range(owned):
        scale_ref[m] = jnp.broadcast_to(scale[m : m + 1, :], (rows, 128))
    rate = outer_rate * (1.0 + outer_momentum)
    for d, piece in zip(order, pieces, strict=True):
        for r in range(CAP):
            m = module_ref[(me ^ d) * (CAP + 1) + r]
            step = rate * scale_ref[m][:, :1]
            for c in chunks(width):
                piece[r, :, c] = (base_ref[m, :, c] - step * acc_ref[m, :, c]).astype(
                    jnp.bfloat16
                )


def store_kernel(distances, places_ref, scale_ref, acc_ref, base_ref, past_ref, *rest):
    n = len(distances)
    pieces, (updated_hbm, velocity_hbm, out_hbm) = rest[:n], rest[n : n + 3]
    updated_ref, velocity_ref, sems, piece_sems = rest[n + 3 :]
    placed(distances, pieces, places_ref, out_hbm, piece_sems, start)
    rate = outer_rate * (1.0 + outer_momentum)
    owned, _, width = acc_ref.shape
    parts = math.gcd(owned, PARTS)
    part = owned // parts

    def copies(i):
        at = pl.ds(i * part, part)
        return [
            pltpu.make_async_copy(ref.at[at], hbm.at[at], sems.at[n, i])
            for n, (ref, hbm) in enumerate(
                ((updated_ref, updated_hbm), (velocity_ref, velocity_hbm))
            )
        ]

    for i in range(parts):

        def fill(m, _):
            scale = scale_ref[m][:, :1]
            for c in chunks(width):
                delta = scale * acc_ref[m, :, c]
                updated_ref[m, :, c] = base_ref[m, :, c] - rate * delta
                velocity_ref[m, :, c] = outer_momentum * past_ref[m, :, c] + delta
            return 0

        lax.fori_loop(i * part, (i + 1) * part, fill, 0)
        for copy in copies(i):
            copy.start()
    for i in range(parts):
        for copy in copies(i):
            copy.wait()
    placed(distances, pieces, places_ref, out_hbm, piece_sems, wait)


def placed(distances, pieces, places_ref, out_ref, sems, act):
    me = lax.axis_index("path").astype(jnp.int32)
    for n, (d, piece) in enumerate(zip(distances, pieces, strict=True)):
        for r in range(CAP):
            k = places_ref[(me ^ d) * CAP + r]

            @pl.when(k >= 0)
            def _():
                act(pltpu.make_async_copy(piece.at[r], out_ref.at[0, k], sems.at[n * CAP + r]))


def start(copy):
    copy.start()


def wait(copy):
    copy.wait()


def unpack_kernel(distances, places_ref, *rest):
    pieces, (out_ref, sems) = rest[: len(distances)], rest[-2:]
    placed(distances, pieces, places_ref, out_ref, sems, start)
    placed(distances, pieces, places_ref, out_ref, sems, wait)


def on_device(path_params, global_params, momentum, module_ids, token_counts):
    paths, held = module_ids.shape
    owned, rows, width = global_params.shape
    shards = lax.axis_size("shard")
    module_ids, counts = in_hbm(module_ids, token_counts)
    slots = paths * CAP
    piece = pltpu.VMEM((CAP, rows, width), jnp.bfloat16)
    module = jax.ShapeDtypeStruct((owned, rows, width), jnp.float32)
    held_module = pltpu.VMEM(module.shape, module.dtype)
    tables = [
        pltpu.SMEM((paths * (CAP + 1),), jnp.int32),
        pltpu.SMEM((paths * (CAP + 1),), jnp.float32),
        pltpu.SMEM((owned,), jnp.float32),
    ]
    room = [
        pltpu.VMEM(module.shape, module.dtype),
        pltpu.VMEM(module.shape, module.dtype),
        pltpu.SemaphoreType.DMA((2, PARTS)),
    ]
    limits = pltpu.CompilerParams(vmem_limit_bytes=24 * 1024 * 1024)
    far = sorted(range(2, paths, 2), key=lambda d: (-d.bit_count(), d))
    there = far + [d + 1 for d in far[::-1]] + [1]
    back = far + [d + 1 for d in far[-1:] + far[:-1]] + [1]

    def exchange(order, pieces):
        return [
            lax.ppermute(x, "path", [(i, i ^ d) for i in range(paths)])
            for d, x in zip(order, pieces)
        ]

    places, *packed = pl.pallas_call(
        functools.partial(pack_kernel, owned, [*there, 0]),
        out_shape=[pltpu.SMEM((slots,), jnp.int32)] + [piece] * paths,
        in_specs=[ANY] * 2,
        out_specs=[SMEM] + [VMEM] * paths,
        scratch_shapes=[
            pltpu.SMEM(module_ids.shape, jnp.int32),
            pltpu.VMEM((held, rows, width), jnp.bfloat16),
            pltpu.SMEM((paths,), jnp.int32),
            pltpu.SemaphoreType.DMA((len(chunks(width)) + 1,)),
        ],
        compiler_params=limits,
        name="pack",
    )(module_ids, *in_hbm(path_params.reshape(held, rows, width)))

    arrived = exchange(there, packed)
    table, weights, total, acc, base = pl.pallas_call(
        early_kernel,
        out_shape=tables + [held_module] * 2,
        in_specs=[SMEM] * 2 + [VMEM] + [ANY] * 2,
        out_specs=[SMEM] * 3 + [VMEM] * 2,
        scratch_shapes=room,
        compiler_params=limits,
        cost_estimate=pl.CostEstimate(flops=10**6, bytes_accessed=12 * 2**20, transcendentals=0),
        name="early",
    )(module_ids, counts, *in_vmem(packed[-1]), *in_hbm(global_params, momentum))
    acc, squares = pl.pallas_call(
        functools.partial(combine_kernel, there),
        out_shape=[held_module, jax.ShapeDtypeStruct((1, 128), jnp.float32)],
        in_specs=[SMEM] * 3 + [VMEM] * paths,
        out_specs=[VMEM] * 2,
        input_output_aliases={3: 0},
        compiler_params=limits,
        name="combine",
    )(*in_smem(table, weights, total), *in_vmem(acc, *arrived))
    parts = [squares] + [
        lax.ppermute(squares, "shard", [(i, (i + d) % shards) for i in range(shards)])
        for d in sorted(range(1, shards), key=lambda d: (d == 2, -d))
    ]
    scale, *outgoing = pl.pallas_call(
        functools.partial(send_kernel, [*back, 0], shards),
        out_shape=[jax.ShapeDtypeStruct((owned, rows, 128), jnp.float32)] + [piece] * paths,
        in_specs=[SMEM] * 2 + [VMEM] * (2 + shards),
        out_specs=[VMEM] * (1 + paths),
        compiler_params=limits,
        name="send",
    )(*in_smem(table, total), *in_vmem(acc, base), *parts)
    returned = {0: outgoing[-1], **dict(zip(back, exchange(back, outgoing)))}
    soon, last = [0, *back[:SOON]], back[SOON:]
    whole = jax.ShapeDtypeStruct(path_params.shape, path_params.dtype)
    updated, velocity, path_out = pl.pallas_call(
        functools.partial(store_kernel, soon),
        out_shape=[module] * 2 + [whole],
        in_specs=[SMEM] + [VMEM] * (4 + len(soon)),
        out_specs=[ANY] * 3,
        scratch_shapes=room + [pltpu.SemaphoreType.DMA((len(soon) * CAP,))],
        compiler_params=limits,
        cost_estimate=pl.CostEstimate(flops=10**6, bytes_accessed=12 * 2**20, transcendentals=0),
        name="store",
    )(
        *in_smem(places), scale, *in_vmem(acc, base), momentum,
        *in_vmem(*[returned[d] for d in soon]),
    )
    path_out = pl.pallas_call(
        functools.partial(unpack_kernel, last),
        out_shape=whole,
        in_specs=[SMEM] + [VMEM] * len(last) + [ANY],
        out_specs=ANY,
        input_output_aliases={1 + len(last): 0},
        scratch_shapes=[pltpu.SemaphoreType.DMA((len(last) * CAP,))],
        name="unpack",
    )(*in_smem(places), *in_vmem(*[returned[d] for d in last]), path_out)
    return updated, velocity, path_out


def solution(mesh):
    placed = (
        P("path", None, "shard", None),
        P("path", "shard", None),
        P("path", "shard", None),
        P(),
        P(),
    )
    return jax.shard_map(
        on_device,
        mesh=mesh,
        in_specs=placed,
        out_specs=(
            P("path", "shard", None),
            P("path", "shard", None),
            P("path", None, "shard", None),
        ),
        check_vma=False,
    )
```
